32 devices in a mesh: gx: 8 (over y, x, core), gy: 4 (over z).
Axes of the slice: x: 2, y: 2, z: 4, core: 2. Of those that a mesh axis runs over, the one named last changes fastest.
Arguments:
- adjoint_start: float32 [2, 4, 2048, 1024], P(None, None, 'gx', 'gy'), may hold values from -6 to 6
- viscosity: float32 [4, 2048, 1024], P(None, 'gx', 'gy'), may hold values from 0.25 to 4
- base_velocity: float32 [2, 2048, 1024], P(None, 'gx', 'gy'), may hold values from -6 to 6
- surface_velocity: float32 [2, 2048, 1024], P(None, 'gx', 'gy'), may hold values from -6 to 6
- ice_mask: int32 [16, 8], P('gx', 'gy'), may hold values 0 or 1
- log_friction: float32 [2048, 1024], P(('gx', 'gy')), may hold values from -1 to 1
- observed_velocity: float32 [2, 2048, 1024], P(None, ('gx', 'gy')), may hold values from -6 to 6
- obs_weight: float32 [2, 2048, 1024], P(None, ('gx', 'gy')), may hold values from 0.2 to 2
Outputs:
- gradient: float32 [2048, 1024], P(('gx', 'gy'))
- adjoint: float32 [2, 4, 2048, 1024], P(None, None, 'gx', 'gy')
The draws below stay inside these ranges and needn't reach their ends.
All inputs are finite; a program needn't handle non-finite values. No bound on the sum of `ice_mask` on one device may be relied on, other than what follows from the above.
Results may differ from the reference program's by a relative error of at most 0.00002.
Values sent between devices are 32-bit elements; how exact they have to be, the bound alone decides.
No kernel may reach another device: no remote copies, remote signals or barrier semaphores. Data moves between devices by JAX's collectives and lax.ppermute only.
A program may use at most 128 MiB of HBM per device.

```python
import math
import jax
import jax.numpy as jnp

LAYERS = 4
SWEEPS = 4
BLOCK = 128
NX = 2048
NY = 1024
NBX = 16
NBY = 8


def with_ends(result, key, smallest, top_value):
    longest = result.shape.index(max(result.shape))
    spots = []
    for shift in (0, 1):
        where = [jax.random.randint(jax.random.fold_in(key, axis), (), 0, length) for axis, length in enumerate(result.shape)]
        where[longest] = (where[longest] + shift) % result.shape[longest]
        spots.append(tuple(where))
    return result.at[spots[0]].set(smallest).at[spots[1]].set(top_value)


def levels(own_key, extent, pieces, smallest, high):
    def one(position, blocks):
        steps = jax.random.uniform(jax.random.fold_in(jax.random.fold_in(own_key, 6), position), (blocks,), jnp.float32, smallest / len(pieces), high / len(pieces))
        return jnp.repeat(jnp.exp(steps), extent[position] // blocks).reshape((-1,) + (1,) * (len(extent) - position - 1))

    level = one(*pieces[0])
    for cut in pieces[1:]:
        level = level * one(*cut)
    return level


def normal_values(key, shape, spread, bound, shards=(), held_as=jnp.bfloat16):
    gain = levels(key, shape, shards, -0.22, 0.18) if shards else 1.0
    entries = jax.random.normal(key, shape, jnp.float32) * spread * gain
    return jnp.minimum(jnp.maximum(entries, -bound), bound).astype(held_as)


def setup_inputs(seed: int = 0) -> dict:
    streams_of = jax.random.split(jax.random.key(seed), 9)
    adjoint_start = normal_values(streams_of[0], (2, LAYERS, NX, NY), 1.0, 6.0, ((2, 8), (3, 4)), jnp.float32)
    viscosity = jnp.clip(jnp.exp(math.log(4.0) - 2.7725887 * jax.random.uniform(streams_of[1], (LAYERS, NX, NY), jnp.float32) ** levels(streams_of[1], (LAYERS, NX, NY), ((1, 8), (2, 4)), -0.2, 0.2)), 0.25, 4.0)
    base_velocity = normal_values(streams_of[2], (2, NX, NY), 1.0, 6.0, ((1, 8), (2, 4)), jnp.float32)
    surface_velocity = normal_values(streams_of[3], (2, NX, NY), 1.0, 6.0, ((1, 8), (2, 4)), jnp.float32)
    ice_mask = with_ends((jax.random.randint(streams_of[4], (NBX, NBY), 0, 4) < 3).astype(jnp.int32), jax.random.fold_in(streams_of[4], 1), 0, 1)
    log_friction = jnp.clip(jax.random.uniform(streams_of[5], (NX, NY), jnp.float32, -1.0, 1.0) * levels(streams_of[5], (NX, NY), ((0, 32),), -0.4, 0.0), -1.0, 1.0)
    observed_velocity = normal_values(streams_of[6], (2, NX, NY), 1.0, 6.0, ((1, 32),), jnp.float32)
    obs_weight = jnp.clip(jnp.exp(math.log(2.0) - 2.3025851 * jax.random.uniform(streams_of[7], (2, NX, NY), jnp.float32) ** levels(streams_of[7], (2, NX, NY), ((1, 32),), -0.2, 0.2)), 0.2, 2.0)
    return dict(adjoint_start=adjoint_start, viscosity=viscosity, base_velocity=base_velocity, surface_velocity=surface_velocity, ice_mask=ice_mask, log_friction=log_friction, observed_velocity=observed_velocity, obs_weight=obs_weight)


DAMPING = 0.8
VERTICAL = 2.0
COUPLING = 3.0
TIKHONOV = 0.25


def relax_once(padded_state, padded_visc, fields):
    friction, force_u, force_v, ice_cells = fields
    centre = padded_visc[:, 1:-1, 1:-1]
    east_face = 0.5 * (centre + padded_visc[:, 2:, 1:-1])
    west_face = 0.5 * (centre + padded_visc[:, :-2, 1:-1])
    north_face = 0.5 * (centre + padded_visc[:, 1:-1, 2:])
    south_face = 0.5 * (centre + padded_visc[:, 1:-1, :-2])
    layer_zero = jnp.zeros_like(centre[:1])
    upper_face = jnp.concatenate([0.5 * (centre[:-1] + centre[1:]), layer_zero], 0)
    lower_face = jnp.concatenate([layer_zero, 0.5 * (centre[1:] + centre[:-1])], 0)
    bed_term = jnp.concatenate([friction[None], jnp.zeros_like(centre[1:])], 0)
    empty_layers = jnp.zeros_like(centre[1:])
    results = []
    for component, along_x, along_y, force in ((0, 4.0, 1.0, force_u), (1, 1.0, 4.0, force_v)):
        own_field = padded_state[component]
        cross_field = padded_state[1 - component]
        middle = own_field[:, 1:-1, 1:-1]
        layer_up = jnp.concatenate([middle[1:], layer_zero], 0)
        layer_down = jnp.concatenate([layer_zero, middle[:-1]], 0)
        face_flux = along_x * (east_face * (middle - own_field[:, 2:, 1:-1]) + west_face * (middle - own_field[:, :-2, 1:-1]))
        face_flux = face_flux + along_y * (north_face * (middle - own_field[:, 1:-1, 2:]) + south_face * (middle - own_field[:, 1:-1, :-2]))
        face_flux = face_flux + VERTICAL * (upper_face * (middle - layer_up) + lower_face * (middle - layer_down)) + bed_term * middle
        mixed_term = 0.25 * (cross_field[:, 2:, 2:] - cross_field[:, 2:, :-2] - cross_field[:, :-2, 2:] + cross_field[:, :-2, :-2])
        applied = face_flux - COUPLING * centre * mixed_term
        diagonal = along_x * (east_face + west_face) + along_y * (north_face + south_face) + VERTICAL * (upper_face + lower_face) + bed_term + COUPLING * centre + (1.0 - ice_cells)
        forcing = jnp.concatenate([empty_layers, force[None]], 0)
        results.append(ice_cells * (middle + DAMPING * (forcing - applied) / diagonal))
    return jnp.stack(results)


def tikhonov_terms(padded, up_present, down_present, left_present, right_present):
    centre = padded[1:-1, 1:-1]
    total = up_present * (centre - padded[:-2, 1:-1]) + down_present * (centre - padded[2:, 1:-1])
    return total + left_present * (centre - padded[1:-1, :-2]) + right_present * (centre - padded[1:-1, 2:])


def reference(adjoint_start, viscosity, base_velocity, surface_velocity, ice_mask, log_friction, observed_velocity, obs_weight):
    friction = jnp.exp(log_friction)
    forcing = obs_weight * (observed_velocity - surface_velocity)
    ice_cells = jnp.repeat(jnp.repeat(ice_mask, BLOCK, axis=0), BLOCK, axis=1).astype(jnp.float32)
    fields = (friction, forcing[0], forcing[1], ice_cells)
    padded_visc = jnp.pad(viscosity, ((0, 0), (1, 1), (1, 1)))
    adjoint = adjoint_start
    for sweep_index in range(SWEEPS):
        adjoint = relax_once(jnp.pad(adjoint, ((0, 0), (0, 0), (1, 1), (1, 1))), padded_visc, fields)
    basal = friction * (base_velocity[0] * adjoint[0, 0] + base_velocity[1] * adjoint[1, 0])
    rows = jnp.arange(NX)[:, None]
    cols = jnp.arange(NY)[None, :]
    up_present = (rows != 0).astype(jnp.float32)
    down_present = (rows != NX - 1).astype(jnp.float32)
    left_present = (cols != 0).astype(jnp.float32)
    right_present = (cols != NY - 1).astype(jnp.float32)
    smoothing = tikhonov_terms(jnp.pad(log_friction, 1), up_present, down_present, left_present, right_present)
    return basal + TIKHONOV * smoothing, adjoint
```

```python
import functools

import jax
import jax.numpy as jnp
from jax import lax
from jax.experimental import pallas as pl
from jax.experimental.pallas import tpu as pltpu
from jax.sharding import PartitionSpec as P

SWEEPS = 4
DAMPING = 0.8
VERTICAL = 2.0
COUPLING = 3.0
TIKHONOV = 0.25

LAYERS = 4
LANES = 128
ROWS = 8
TILE = 256
FRAME = TILE + 2 * ROWS
HALF = TILE // 2
BLOCKS = TILE // ROWS
FIRST = 4
STEPS = BLOCKS + 1
TILE_FIELDS = 15
RIM_FIELDS = 20
VMEM_BYTES = 56 * 1024 * 1024


def lane_index():
    return lax.broadcasted_iota(jnp.int32, (ROWS, LANES), 1)


def roll_to(x, shift):
    shift = shift % LANES
    return x if shift == 0 else pltpu.roll(x, shift, 1)


def after(x, lane):
    a, b, c = (roll_to(v, -1) for v in x)
    last = lane == LANES - 1
    return jnp.where(last, b, a), jnp.where(last, c, b), jnp.where(last, a, c)


def before(x, lane):
    a, b, c = (roll_to(v, 1) for v in x)
    first = lane == 0
    return jnp.where(first, c, a), jnp.where(first, a, b), jnp.where(first, b, c)


def rim_slot(array, block, strip_blocks):
    position = array * strip_blocks + block
    return position // 16, position % 16


def rim_tiles(strip_rows):
    return -(-5 * (strip_rows // ROWS) // 16)


def control_rows(strip_rows):
    return 2 * strip_rows + 64 + ROWS * rim_tiles(strip_rows)


def pack_strips(n, strip_rows, logf, obs, weight, *outs):
    controls, datas = outs[:n], outs[n:]
    me = lax.axis_index("gy")
    lane = lane_index()
    blocks = strip_rows // ROWS
    edge = jnp.where(me == 0, 0, strip_rows - ROWS)
    edge = pl.multiple_of(edge, ROWS)
    strips = [logf.at[...], obs.at[0], obs.at[1], weight.at[0], weight.at[1]]
    width = n * TILE
    for k in range(n):
        to = lax.rem(me + k, n)
        column = pl.multiple_of(to * TILE, TILE)
        left = pl.multiple_of(jnp.maximum(column - LANES, 0), LANES)
        right = pl.multiple_of(jnp.minimum(column + TILE, width - LANES), LANES)
        control, data = controls[k], datas[k]
        for t in range(2):
            columns = pl.ds(column + t * LANES, LANES)
            control[pl.ds(t * strip_rows, strip_rows), :] = logf[:, columns]
            for a in range(4):
                data[a, t] = strips[a + 1][:, columns]
                control[pl.ds(2 * strip_rows + (a * 2 + t) * ROWS, ROWS), :] = strips[a + 1][pl.ds(edge, ROWS), columns]
        packed = [jnp.zeros((ROWS, LANES), jnp.float32) for _ in range(rim_tiles(strip_rows))]
        for a in range(5):
            for b in range(blocks):
                part, slot = rim_slot(a, b, blocks)
                rows = pl.ds(b * ROWS, ROWS)
                both = jnp.where(lane < 64, strips[a][rows, pl.ds(right, LANES)], strips[a][rows, pl.ds(left, LANES)])
                packed[part] = jnp.where(lane // 8 == slot, roll_to(both, 8 * slot + 4), packed[part])
        for part, value in enumerate(packed):
            control[pl.ds(2 * strip_rows + 64 + part * ROWS, ROWS), :] = value


def tile_field(a, adjoint, viscosity, surface):
    if a < 8:
        return adjoint.at[a]
    if a < 12:
        return viscosity.at[a - 8]
    return surface.at[a - 12]


def pack_columns(mask, adjoint, viscosity, surface, up, down):
    lane = lane_index()

    def step(r, carry):
        to_up = jnp.zeros((ROWS, LANES), jnp.float32)
        to_down = jnp.zeros((ROWS, LANES), jnp.float32)
        for h in range(2):
            rows = pl.ds(pl.multiple_of(h * HALF + r * ROWS, ROWS), ROWS)
            for a in range(TILE_FIELDS):
                slot = h * TILE_FIELDS + a
                here = lane // 4 == slot
                if a == TILE_FIELDS - 1:
                    low = mask[h, 0].astype(jnp.float32)
                    high = mask[h, 1].astype(jnp.float32)
                    to_up = jnp.where(here, high, to_up)
                    to_down = jnp.where(here, low, to_down)
                else:
                    field = tile_field(a, adjoint, viscosity, surface)
                    to_up = jnp.where(here, roll_to(field[rows, LANES:], 4 * slot + 4), to_up)
                    to_down = jnp.where(here, roll_to(field[rows, :LANES], 4 * slot), to_down)
        rows = pl.ds(pl.multiple_of(r * ROWS, ROWS), ROWS)
        up[rows, :] = to_up
        down[rows, :] = to_down
        return carry

    lax.fori_loop(0, HALF // ROWS, step, 0)


def side_columns(lane, from_left, from_right, slot):
    left = roll_to(from_left, -(4 * slot + 4))
    right = roll_to(from_right, -4 * slot)
    return jnp.where(lane < 4, right, jnp.where(lane >= LANES - 4, left, 0.0))


def strip_columns(lane, packed, slot):
    value = roll_to(packed, -(8 * slot + 4))
    return jnp.where(jnp.logical_or(lane < 4, lane >= LANES - 4), value, 0.0)


def pack_rows(n, strip_rows, mask, adjoint, viscosity, surface, from_left, from_right, *rest):
    controls, (up, down) = rest[:n], rest[n:]
    me = lax.axis_index("gy")
    lane = lane_index()
    blocks = strip_rows // ROWS
    for message, h, row, owner in ((up, 1, TILE - ROWS, n - 1), (down, 0, 0, 0)):
        rows = pl.ds(row, ROWS)
        packed_rows = pl.ds(row - h * HALF, ROWS)
        left, right = from_left[packed_rows, :], from_right[packed_rows, :]
        for a in range(TILE_FIELDS):
            for t in range(2):
                if a == TILE_FIELDS - 1:
                    message[a, t] = jnp.full((ROWS, LANES), mask[h, t].astype(jnp.float32))
                else:
                    message[a, t] = tile_field(a, adjoint, viscosity, surface)[rows, t * LANES : (t + 1) * LANES]
            message[a, 2] = side_columns(lane, left, right, h * TILE_FIELDS + a)
        block = blocks - 1 if h else 0
        for k in range(n):

            @pl.when(lax.rem(me - k + n, n) == owner)
            def _():
                control = controls[k]
                for a in range(5):
                    for t in range(2):
                        if a == 0:
                            start = t * strip_rows + block * ROWS
                        else:
                            start = 2 * strip_rows + ((a - 1) * 2 + t) * ROWS
                        message[TILE_FIELDS + a, t] = control[pl.ds(start, ROWS), :]
                    part, slot = rim_slot(a, block, blocks)
                    packed = control[pl.ds(2 * strip_rows + 64 + part * ROWS, ROWS), :]
                    message[TILE_FIELDS + a, 2] = strip_columns(lane, packed, slot)


E_, N_, S_, U_, V_, K0_, K1_, I0_, I1_ = range(9)


def coefficients(coef, visc, fric, ice, lane):
    def step(i, carry):
        r = FIRST + i * ROWS
        rows, east, west = pl.ds(r, ROWS), pl.ds(r + 1, ROWS), pl.ds(r - 1, ROWS)
        cells = [ice[t, rows, :] for t in range(3)]
        layers = [[visc[l, t, rows, :] for t in range(3)] for l in range(LAYERS)]
        for l in range(LAYERS):
            centre = layers[l]
            north, south = after(centre, lane), before(centre, lane)
            for t in range(3):
                c = centre[t]
                e = 0.5 * (c + visc[l, t, east, :])
                w = 0.5 * (c + visc[l, t, west, :])
                nf = 0.5 * (c + north[t])
                sf = 0.5 * (c + south[t])
                coef[l, E_, t, rows, :] = e
                coef[l, N_, t, rows, :] = nf
                coef[l, S_, t, rows, :] = sf
                vertical = None
                if l < LAYERS - 1:
                    u = (0.5 * VERTICAL) * (c + layers[l + 1][t])
                    coef[l, U_, t, rows, :] = u
                    vertical = u
                if l > 0:
                    lower = (0.5 * VERTICAL) * (c + layers[l - 1][t])
                    vertical = lower if vertical is None else vertical + lower
                if l == 0:
                    vertical = vertical + fric[t, rows, :]
                coef[l, V_, t, rows, :] = (0.25 * COUPLING) * c
                rest = COUPLING * c + (1.0 - cells[t])
                ew, ns = e + w, nf + sf
                for c_, ax, ay in ((0, 4.0, 1.0), (1, 1.0, 4.0)):
                    own = (ax * ew if ax != 1.0 else ew) + (ay * ns if ay != 1.0 else ns) + vertical
                    inverse = DAMPING * cells[t] / (own + rest)
                    coef[l, I0_ + c_, t, rows, :] = inverse
                    coef[l, K0_ + c_, t, rows, :] = cells[t] - own * inverse
        return carry

    lax.fori_loop(0, STEPS, step, 0)


def sweep_layer(coef, old, new, l, lane, force=None):
    def step(i, carry):
        r = FIRST + i * ROWS
        rows, east, west = pl.ds(r, ROWS), pl.ds(r + 1, ROWS), pl.ds(r - 1, ROWS)
        e = [coef[l, E_, t, rows, :] for t in range(3)]
        w = [coef[l, E_, t, west, :] for t in range(3)]
        fluxes, mixes = [], []
        for c in range(2):
            m = [old[c * LAYERS + l, t, rows, :] for t in range(3)]
            me = [old[c * LAYERS + l, t, east, :] for t in range(3)]
            mw = [old[c * LAYERS + l, t, west, :] for t in range(3)]
            mn, ms = after(m, lane), before(m, lane)
            across = [me[t] - mw[t] for t in range(3)]
            an, as_ = after(across, lane), before(across, lane)
            mixes.append([an[t] - as_[t] for t in range(3)])
            flux = []
            for t in range(3):
                x = e[t] * me[t] + w[t] * mw[t]
                y = coef[l, N_, t, rows, :] * mn[t] + coef[l, S_, t, rows, :] * ms[t]
                total = 4.0 * x + y if c == 0 else x + 4.0 * y
                if l < LAYERS - 1:
                    total = total + coef[l, U_, t, rows, :] * old[c * LAYERS + l + 1, t, rows, :]
                if l > 0:
                    total = total + coef[l - 1, U_, t, rows, :] * old[c * LAYERS + l - 1, t, rows, :]
                if force is not None:
                    total = total + force[c, t, rows, :]
                flux.append((total, m[t]))
            fluxes.append(flux)
        for c in range(2):
            for t in range(3):
                total, m = fluxes[c][t]
                total = total + coef[l, V_, t, rows, :] * mixes[1 - c][t]
                new[c * LAYERS + l, t, rows, :] = (
                    coef[l, K0_ + c, t, rows, :] * m + coef[l, I0_ + c, t, rows, :] * total
                )
        return carry

    lax.fori_loop(0, STEPS, step, 0)


def sweeps_kernel(n, strip_rows, mask, adjoint, viscosity, surface, base, from_left, from_right, above, below, *rest):
    controls, datas = rest[:n], rest[n : 2 * n]
    grads, out = rest[2 * n : 3 * n], rest[3 * n]
    state, other, visc, surf, ice, logf, fric, given, bed, coef, force, grad, packed, sems = rest[3 * n + 1 :]
    me, mx = lax.axis_index("gy"), lax.axis_index("gx")
    size_x = lax.axis_size("gx")
    lane = lane_index()
    blocks = strip_rows // ROWS
    main = pl.ds(ROWS, TILE)
    copies = []

    def start(source, target):
        copy = pltpu.make_async_copy(source, target, sems.at[len(copies)])
        copy.start()
        copies.append(copy)

    for t in range(2):
        columns = pl.ds(t * LANES, LANES)
        start(adjoint.at[:, :, columns], state.at[:, t, main, :])
        start(viscosity.at[:, :, columns], visc.at[:, t, main, :])
        start(surface.at[:, :, columns], surf.at[:, t, main, :])
        start(base.at[:, :, columns], bed.at[:, t])
    for message, row in ((above, 0), (below, ROWS + TILE)):
        rows = pl.ds(row, ROWS)
        start(message.at[0:8], state.at[:, :, rows, :])
        start(message.at[8:12], visc.at[:, :, rows, :])
        start(message.at[12:14], surf.at[:, :, rows, :])
        start(message.at[14], ice.at[:, rows, :])
        start(message.at[15], logf.at[:, rows, :])
        start(message.at[16:20], given.at[:, :, rows, :])
    for k in range(n):
        source = lax.rem(me - k + n, n)
        rows = pl.ds(pl.multiple_of(ROWS + source * strip_rows, ROWS), strip_rows)
        start(controls[k].at[0:strip_rows], logf.at[0, rows, :])
        start(controls[k].at[strip_rows : 2 * strip_rows], logf.at[1, rows, :])
        start(controls[k].at[2 * strip_rows + 64 :], packed.at[k])
        start(datas[k], given.at[:, 0:2, rows, :])
    for copy in copies:
        copy.wait()

    for h in range(2):
        for t in range(2):
            ice[t, pl.ds(ROWS + h * HALF, HALF), :] = jnp.full((HALF, LANES), mask[h, t].astype(jnp.float32))

    def sides(r, carry):
        rows = pl.ds(pl.multiple_of(r * ROWS, ROWS), ROWS)
        left, right = from_left[rows, :], from_right[rows, :]
        for h in range(2):
            to = pl.ds(pl.multiple_of(ROWS + h * HALF + r * ROWS, ROWS), ROWS)
            for a in range(TILE_FIELDS):
                value = side_columns(lane, left, right, h * TILE_FIELDS + a)
                if a < 8:
                    state[a, 2, to, :] = value
                elif a < 12:
                    visc[a - 8, 2, to, :] = value
                elif a < 14:
                    surf[a - 12, 2, to, :] = value
                else:
                    ice[2, to, :] = value
        return carry

    lax.fori_loop(0, HALF // ROWS, sides, 0)
    for k in range(n):
        source = lax.rem(me - k + n, n)
        for a in range(5):
            for b in range(blocks):
                part, slot = rim_slot(a, b, blocks)
                value = strip_columns(lane, packed[k, pl.ds(part * ROWS, ROWS), :], slot)
                to = pl.ds(pl.multiple_of(ROWS + source * strip_rows + b * ROWS, ROWS), ROWS)
                if a == 0:
                    logf[2, to, :] = value
                else:
                    given[a - 1, 2, to, :] = value

    def fields(i, carry):
        rows = pl.ds(pl.multiple_of(i * ROWS, ROWS), ROWS)
        for t in range(3):
            fric[t, rows, :] = jnp.exp(logf[t, rows, :])
            for c in range(2):
                force[c, t, rows, :] = given[2 + c, t, rows, :] * (given[c, t, rows, :] - surf[c, t, rows, :])
        return carry

    lax.fori_loop(0, FRAME // ROWS, fields, 0)
    coefficients(coef, visc, fric, ice, lane)
    old, new = state, other
    for _ in range(SWEEPS):
        for l in range(LAYERS):
            sweep_layer(coef, old, new, l, lane, force if l == LAYERS - 1 else None)
        old, new = new, old
    outs = []
    for t in range(2):
        copy = pltpu.make_async_copy(old.at[:, t, main, :], out.at[:, :, pl.ds(t * LANES, LANES)], sems.at[t])
        copy.start()
        outs.append(copy)

    def finish(i, carry):
        r = pl.multiple_of(i * ROWS, ROWS)
        rows, east, west = pl.ds(r + ROWS, ROWS), pl.ds(r + ROWS + 1, ROWS), pl.ds(r + ROWS - 1, ROWS)
        centre = [logf[t, rows, :] for t in range(3)]
        north, south = after(centre, lane), before(centre, lane)
        row = lax.broadcasted_iota(jnp.int32, (ROWS, LANES), 0) + r
        in_west = jnp.logical_or(row != 0, mx != 0)
        in_east = jnp.logical_or(row != TILE - 1, mx != size_x - 1)
        in_south = jnp.logical_or(lane != 0, me != 0)
        in_north = jnp.logical_or(lane != LANES - 1, me != n - 1)
        for t in range(2):
            c = centre[t]
            smooth = jnp.where(in_west, c - logf[t, west, :], 0.0) + jnp.where(in_east, c - logf[t, east, :], 0.0)
            below_ = c - south[t]
            above_ = c - north[t]
            smooth = smooth + (jnp.where(in_south, below_, 0.0) if t == 0 else below_)
            smooth = smooth + (jnp.where(in_north, above_, 0.0) if t == 1 else above_)
            inner = pl.ds(r, ROWS)
            basal = fric[t, rows, :] * (
                bed[0, t, inner, :] * old[0, t, rows, :] + bed[1, t, inner, :] * old[LAYERS, t, rows, :]
            )
            grad[t, inner, :] = basal + TIKHONOV * smooth
        return carry

    lax.fori_loop(0, BLOCKS, finish, 0)
    for k in range(n):
        to = lax.rem(me + k, n)
        rows = pl.ds(pl.multiple_of(to * strip_rows, ROWS), strip_rows)
        copy = pltpu.make_async_copy(grad.at[:, rows, :], grads[k], sems.at[2 + k])
        copy.start()
        outs.append(copy)
    for copy in outs:
        copy.wait()


def unpack_gradient(n, *refs):
    parts, out = refs[:n], refs[n]
    me = lax.axis_index("gy")
    for k in range(n):
        source = lax.rem(me - k + n, n)
        for t in range(2):
            out[:, pl.ds(pl.multiple_of(source * TILE + t * LANES, LANES), LANES)] = parts[k][t]


def f32(*shape):
    return jax.ShapeDtypeStruct(shape, jnp.float32)


def per_device(
    adjoint_start,
    viscosity,
    base_velocity,
    surface_velocity,
    ice_mask,
    log_friction,
    observed_velocity,
    obs_weight,
):
    n = lax.axis_size("gy")
    size_x = lax.axis_size("gx")
    strip_rows = log_friction.shape[0]
    vmem = pl.BlockSpec(memory_space=pltpu.VMEM)
    smem = pl.BlockSpec(memory_space=pltpu.SMEM)
    anywhere = pl.BlockSpec(memory_space=pl.ANY)
    params = pltpu.CompilerParams(vmem_limit_bytes=VMEM_BYTES)
    adjoint = adjoint_start.reshape((2 * LAYERS, TILE, TILE))

    def ring(k):
        return [(i, (i + k) % n) for i in range(n)]

    def line(size, k):
        return [(i, i + k) for i in range(size) if 0 <= i + k < size]

    packed = pl.pallas_call(
        functools.partial(pack_strips, n, strip_rows),
        out_shape=[f32(control_rows(strip_rows), LANES)] * n + [f32(4, 2, strip_rows, LANES)] * n,
        in_specs=[vmem] * 3,
        out_specs=[vmem] * (2 * n),
        compiler_params=params,
    )(log_friction, observed_velocity, obs_weight)
    controls, datas = packed[:n], packed[n:]
    controls = [controls[0]] + [lax.ppermute(controls[k], "gy", ring(k)) for k in range(1, n)]
    datas = [datas[0]] + [lax.ppermute(datas[k], "gy", ring(k)) for k in range(1, n)]

    columns_up, columns_down = pl.pallas_call(
        pack_columns,
        out_shape=[f32(HALF, LANES)] * 2,
        in_specs=[smem, vmem, vmem, vmem],
        out_specs=[vmem] * 2,
        compiler_params=params,
    )(ice_mask, adjoint, viscosity, surface_velocity)
    from_left = lax.ppermute(columns_up, "gy", line(n, 1))
    from_right = lax.ppermute(columns_down, "gy", line(n, -1))

    rows_up, rows_down = pl.pallas_call(
        functools.partial(pack_rows, n, strip_rows),
        out_shape=[f32(RIM_FIELDS, 3, ROWS, LANES)] * 2,
        in_specs=[smem] + [vmem] * (5 + n),
        out_specs=[vmem] * 2,
        compiler_params=params,
    )(ice_mask, adjoint, viscosity, surface_velocity, from_left, from_right, *controls)
    above = lax.ppermute(rows_up, "gx", line(size_x, 1))
    below = lax.ppermute(rows_down, "gx", line(size_x, -1))

    def frames(*leading):
        return pltpu.VMEM(leading + (3, FRAME, LANES), jnp.float32)

    *grads, out = pl.pallas_call(
        functools.partial(sweeps_kernel, n, strip_rows),
        out_shape=[f32(2, strip_rows, LANES)] * n + [f32(2 * LAYERS, TILE, TILE)],
        in_specs=[smem] + [anywhere] * 4 + [vmem] * 2 + [anywhere] * (2 + 2 * n),
        out_specs=[anywhere] * (n + 1),
        scratch_shapes=[
            frames(8),
            frames(8),
            frames(4),
            frames(2),
            frames(),
            frames(),
            frames(),
            frames(4),
            pltpu.VMEM((2, 2, TILE, LANES), jnp.float32),
            frames(LAYERS, 9),
            frames(2),
            pltpu.VMEM((2, TILE, LANES), jnp.float32),
            pltpu.VMEM((n, ROWS * rim_tiles(strip_rows), LANES), jnp.float32),
            pltpu.SemaphoreType.DMA((20 + 4 * n,)),
        ],
        compiler_params=params,
    )(
        ice_mask,
        adjoint,
        viscosity,
        surface_velocity,
        base_velocity,
        from_left,
        from_right,
        above,
        below,
        *controls,
        *datas,
    )
    parts = [grads[0]] + [lax.ppermute(grads[k], "gy", ring(k)) for k in range(1, n)]
    gradient = pl.pallas_call(
        functools.partial(unpack_gradient, n),
        out_shape=f32(strip_rows, n * TILE),
        in_specs=[vmem] * n,
        out_specs=vmem,
        compiler_params=params,
    )(*parts)
    return gradient, out.reshape(adjoint_start.shape)


def solution(mesh):
    placed = (
        P(None, None, "gx", "gy"),
        P(None, "gx", "gy"),
        P(None, "gx", "gy"),
        P(None, "gx", "gy"),
        P("gx", "gy"),
        P(("gx", "gy"), None),
        P(None, ("gx", "gy"), None),
        P(None, ("gx", "gy"), None),
    )
    return jax.shard_map(
        per_device,
        mesh=mesh,
        in_specs=placed,
        out_specs=(P(("gx", "gy"), None), P(None, None, "gx", "gy")),
        check_vma=False,
    )
```

```python
import functools

import jax
import jax.numpy as jnp
from jax import lax
from jax.experimental import pallas as pl
from jax.experimental.pallas import tpu as pltpu
from jax.sharding import PartitionSpec as P

SWEEPS = 4
DAMPING = 0.8
VERTICAL = 2.0
COUPLING = 3.0
TIKHONOV = 0.25

LAYERS = 4
LANES = 128
ROWS = 8
TILE = 256
FRAME = TILE + 2 * ROWS
HALF = TILE // 2
BLOCKS = TILE // ROWS
FIRST = 4
STEPS = BLOCKS + 1
TILE_FIELDS = 15
RIM_FIELDS = 20
VMEM_BYTES = 56 * 1024 * 1024


def lane_index():
    return lax.broadcasted_iota(jnp.int32, (ROWS, LANES), 1)


def roll_to(x, shift):
    shift = shift % LANES
    return x if shift == 0 else pltpu.roll(x, shift, 1)


def after(x, lane):
    a, b, c = (roll_to(v, -1) for v in x)
    last = lane == LANES - 1
    return jnp.where(last, b, a), jnp.where(last, c, b), jnp.where(last, a, c)


def before(x, lane):
    a, b, c = (roll_to(v, 1) for v in x)
    first = lane == 0
    return jnp.where(first, c, a), jnp.where(first, a, b), jnp.where(first, b, c)


def rim_slot(array, block, strip_blocks):
    position = array * strip_blocks + block
    return position // 16, position % 16


def rim_tiles(strip_rows):
    return -(-5 * (strip_rows // ROWS) // 16)


def control_rows(strip_rows):
    return 2 * strip_rows + 64 + ROWS * rim_tiles(strip_rows)


def pack_strips(n, strip_rows, logf, obs, weight, *outs):
    controls, datas = outs[:n], outs[n:]
    me = lax.axis_index("gy")
    lane = lane_index()
    blocks = strip_rows // ROWS
    edge = jnp.where(me == 0, 0, strip_rows - ROWS)
    edge = pl.multiple_of(edge, ROWS)
    strips = [logf.at[...], obs.at[0], obs.at[1], weight.at[0], weight.at[1]]
    width = n * TILE
    for k in range(n):
        to = lax.rem(me + k, n)
        column = pl.multiple_of(to * TILE, TILE)
        left = pl.multiple_of(jnp.maximum(column - LANES, 0), LANES)
        right = pl.multiple_of(jnp.minimum(column + TILE, width - LANES), LANES)
        control, data = controls[k], datas[k]
        for t in range(2):
            columns = pl.ds(column + t * LANES, LANES)
            control[pl.ds(t * strip_rows, strip_rows), :] = logf[:, columns]
            for a in range(4):
                data[a, t] = strips[a + 1][:, columns]
                control[pl.ds(2 * strip_rows + (a * 2 + t) * ROWS, ROWS), :] = strips[a + 1][pl.ds(edge, ROWS), columns]
        packed = [jnp.zeros((ROWS, LANES), jnp.float32) for _ in range(rim_tiles(strip_rows))]
        for a in range(5):
            for b in range(blocks):
                part, slot = rim_slot(a, b, blocks)
                rows = pl.ds(b * ROWS, ROWS)
                both = jnp.where(lane < 64, strips[a][rows, pl.ds(right, LANES)], strips[a][rows, pl.ds(left, LANES)])
                packed[part] = jnp.where(lane // 8 == slot, roll_to(both, 8 * slot + 4), packed[part])
        for part, value in enumerate(packed):
            control[pl.ds(2 * strip_rows + 64 + part * ROWS, ROWS), :] = value


def tile_field(a, adjoint, viscosity, surface):
    if a < 8:
        return adjoint.at[a]
    if a < 12:
        return viscosity.at[a - 8]
    return surface.at[a - 12]


def pack_columns(mask, adjoint, viscosity, surface, up, down):
    lane = lane_index()

    def step(r, carry):
        to_up = jnp.zeros((ROWS, LANES), jnp.float32)
        to_down = jnp.zeros((ROWS, LANES), jnp.float32)
        for h in range(2):
            rows = pl.ds(pl.multiple_of(h * HALF + r * ROWS, ROWS), ROWS)
            for a in range(TILE_FIELDS):
                slot = h * TILE_FIELDS + a
                here = lane // 4 == slot
                if a == TILE_FIELDS - 1:
                    low = mask[h, 0].astype(jnp.float32)
                    high = mask[h, 1].astype(jnp.float32)
                    to_up = jnp.where(here, high, to_up)
                    to_down = jnp.where(here, low, to_down)
                else:
                    field = tile_field(a, adjoint, viscosity, surface)
                    to_up = jnp.where(here, roll_to(field[rows, LANES:], 4 * slot + 4), to_up)
                    to_down = jnp.where(here, roll_to(field[rows, :LANES], 4 * slot), to_down)
        rows = pl.ds(pl.multiple_of(r * ROWS, ROWS), ROWS)
        up[rows, :] = to_up
        down[rows, :] = to_down
        return carry

    lax.fori_loop(0, HALF // ROWS, step, 0, unroll=4)


def side_columns(lane, from_left, from_right, slot):
    left = roll_to(from_left, -(4 * slot + 4))
    right = roll_to(from_right, -4 * slot)
    return jnp.where(lane < 4, right, jnp.where(lane >= LANES - 4, left, 0.0))


def strip_columns(lane, packed, slot):
    value = roll_to(packed, -(8 * slot + 4))
    return jnp.where(jnp.logical_or(lane < 4, lane >= LANES - 4), value, 0.0)


def pack_rows(n, strip_rows, mask, adjoint, viscosity, surface, from_left, from_right, *rest):
    controls, (up, down) = rest[:n], rest[n:]
    me = lax.axis_index("gy")
    lane = lane_index()
    blocks = strip_rows // ROWS
    for message, h, row, owner in ((up, 1, TILE - ROWS, n - 1), (down, 0, 0, 0)):
        rows = pl.ds(row, ROWS)
        packed_rows = pl.ds(row - h * HALF, ROWS)
        left, right = from_left[packed_rows, :], from_right[packed_rows, :]
        for a in range(TILE_FIELDS):
            for t in range(2):
                if a == TILE_FIELDS - 1:
                    message[a, t] = jnp.full((ROWS, LANES), mask[h, t].astype(jnp.float32))
                else:
                    message[a, t] = tile_field(a, adjoint, viscosity, surface)[rows, t * LANES : (t + 1) * LANES]
            message[a, 2] = side_columns(lane, left, right, h * TILE_FIELDS + a)
        block = blocks - 1 if h else 0
        for k in range(n):

            @pl.when(lax.rem(me - k + n, n) == owner)
            def _():
                control = controls[k]
                for a in range(5):
                    for t in range(2):
                        if a == 0:
                            start = t * strip_rows + block * ROWS
                        else:
                            start = 2 * strip_rows + ((a - 1) * 2 + t) * ROWS
                        message[TILE_FIELDS + a, t] = control[pl.ds(start, ROWS), :]
                    part, slot = rim_slot(a, block, blocks)
                    packed = control[pl.ds(2 * strip_rows + 64 + part * ROWS, ROWS), :]
                    message[TILE_FIELDS + a, 2] = strip_columns(lane, packed, slot)


E_, N_, S_, U_, V_, K0_, K1_, I0_, I1_ = range(9)


def coefficients(coef, visc, fric, ice, lane):
    def step(i, carry):
        r = FIRST + i * ROWS
        rows, east, west = pl.ds(r, ROWS), pl.ds(r + 1, ROWS), pl.ds(r - 1, ROWS)
        cells = [ice[t, rows, :] for t in range(3)]
        layers = [[visc[l, t, rows, :] for t in range(3)] for l in range(LAYERS)]
        for l in range(LAYERS):
            centre = layers[l]
            north, south = after(centre, lane), before(centre, lane)
            for t in range(3):
                c = centre[t]
                e = 0.5 * (c + visc[l, t, east, :])
                w = 0.5 * (c + visc[l, t, west, :])
                nf = 0.5 * (c + north[t])
                sf = 0.5 * (c + south[t])
                coef[l, E_, t, rows, :] = e
                coef[l, N_, t, rows, :] = nf
                coef[l, S_, t, rows, :] = sf
                vertical = None
                if l < LAYERS - 1:
                    u = (0.5 * VERTICAL) * (c + layers[l + 1][t])
                    coef[l, U_, t, rows, :] = u
                    vertical = u
                if l > 0:
                    lower = (0.5 * VERTICAL) * (c + layers[l - 1][t])
                    vertical = lower if vertical is None else vertical + lower
                if l == 0:
                    vertical = vertical + fric[t, rows, :]
                coef[l, V_, t, rows, :] = (0.25 * COUPLING) * c
                rest = COUPLING * c + (1.0 - cells[t])
                ew, ns = e + w, nf + sf
                for c_, ax, ay in ((0, 4.0, 1.0), (1, 1.0, 4.0)):
                    own = (ax * ew if ax != 1.0 else ew) + (ay * ns if ay != 1.0 else ns) + vertical
                    inverse = DAMPING * cells[t] / (own + rest)
                    coef[l, I0_ + c_, t, rows, :] = inverse
                    coef[l, K0_ + c_, t, rows, :] = cells[t] - own * inverse
        return carry

    lax.fori_loop(0, STEPS, step, 0, unroll=STEPS)


def sweep_layer(coef, old, new, l, lane, force=None):
    def step(i, carry):
        r = FIRST + i * ROWS
        rows, east, west = pl.ds(r, ROWS), pl.ds(r + 1, ROWS), pl.ds(r - 1, ROWS)
        e = [coef[l, E_, t, rows, :] for t in range(3)]
        w = [coef[l, E_, t, west, :] for t in range(3)]
        fluxes, mixes = [], []
        for c in range(2):
            m = [old[c * LAYERS + l, t, rows, :] for t in range(3)]
            me = [old[c * LAYERS + l, t, east, :] for t in range(3)]
            mw = [old[c * LAYERS + l, t, west, :] for t in range(3)]
            mn, ms = after(m, lane), before(m, lane)
            across = [me[t] - mw[t] for t in range(3)]
            an, as_ = after(across, lane), before(across, lane)
            mixes.append([an[t] - as_[t] for t in range(3)])
            flux = []
            for t in range(3):
                x = e[t] * me[t] + w[t] * mw[t]
                y = coef[l, N_, t, rows, :] * mn[t] + coef[l, S_, t, rows, :] * ms[t]
                total = 4.0 * x + y if c == 0 else x + 4.0 * y
                if l < LAYERS - 1:
                    total = total + coef[l, U_, t, rows, :] * old[c * LAYERS + l + 1, t, rows, :]
                if l > 0:
                    total = total + coef[l - 1, U_, t, rows, :] * old[c * LAYERS + l - 1, t, rows, :]
                if force is not None:
                    total = total + force[c, t, rows, :]
                flux.append((total, m[t]))
            fluxes.append(flux)
        for c in range(2):
            for t in range(3):
                total, m = fluxes[c][t]
                total = total + coef[l, V_, t, rows, :] * mixes[1 - c][t]
                new[c * LAYERS + l, t, rows, :] = (
                    coef[l, K0_ + c, t, rows, :] * m + coef[l, I0_ + c, t, rows, :] * total
                )
        return carry

    lax.fori_loop(0, STEPS, step, 0, unroll=STEPS)


def sweeps_kernel(n, strip_rows, mask, adjoint, viscosity, surface, base, from_left, from_right, above, below, *rest):
    controls, datas = rest[:n], rest[n : 2 * n]
    grads, out = rest[2 * n : 3 * n], rest[3 * n]
    state, other, visc, surf, ice, logf, fric, given, bed, coef, force, grad, packed, sems = rest[3 * n + 1 :]
    me, mx = lax.axis_index("gy"), lax.axis_index("gx")
    size_x = lax.axis_size("gx")
    lane = lane_index()
    blocks = strip_rows // ROWS
    main = pl.ds(ROWS, TILE)
    copies = []

    def start(source, target):
        copy = pltpu.make_async_copy(source, target, sems.at[len(copies)])
        copy.start()
        copies.append(copy)

    for t in range(2):
        columns = pl.ds(t * LANES, LANES)
        start(adjoint.at[:, :, columns], state.at[:, t, main, :])
        start(viscosity.at[:, :, columns], visc.at[:, t, main, :])
        start(surface.at[:, :, columns], surf.at[:, t, main, :])
        start(base.at[:, :, columns], bed.at[:, t])
    for message, row in ((above, 0), (below, ROWS + TILE)):
        rows = pl.ds(row, ROWS)
        start(message.at[0:8], state.at[:, :, rows, :])
        start(message.at[8:12], visc.at[:, :, rows, :])
        start(message.at[12:14], surf.at[:, :, rows, :])
        start(message.at[14], ice.at[:, rows, :])
        start(message.at[15], logf.at[:, rows, :])
        start(message.at[16:20], given.at[:, :, rows, :])
    for k in range(n):
        source = lax.rem(me - k + n, n)
        rows = pl.ds(pl.multiple_of(ROWS + source * strip_rows, ROWS), strip_rows)
        start(controls[k].at[0:strip_rows], logf.at[0, rows, :])
        start(controls[k].at[strip_rows : 2 * strip_rows], logf.at[1, rows, :])
        start(controls[k].at[2 * strip_rows + 64 :], packed.at[k])
        start(datas[k], given.at[:, 0:2, rows, :])
    for copy in copies:
        copy.wait()

    for h in range(2):
        for t in range(2):
            ice[t, pl.ds(ROWS + h * HALF, HALF), :] = jnp.full((HALF, LANES), mask[h, t].astype(jnp.float32))

    def sides(r, carry):
        rows = pl.ds(pl.multiple_of(r * ROWS, ROWS), ROWS)
        left, right = from_left[rows, :], from_right[rows, :]
        for h in range(2):
            to = pl.ds(pl.multiple_of(ROWS + h * HALF + r * ROWS, ROWS), ROWS)
            for a in range(TILE_FIELDS):
                value = side_columns(lane, left, right, h * TILE_FIELDS + a)
                if a < 8:
                    state[a, 2, to, :] = value
                elif a < 12:
                    visc[a - 8, 2, to, :] = value
                elif a < 14:
                    surf[a - 12, 2, to, :] = value
                else:
                    ice[2, to, :] = value
        return carry

    lax.fori_loop(0, HALF // ROWS, sides, 0, unroll=4)
    for k in range(n):
        source = lax.rem(me - k + n, n)
        for a in range(5):
            for b in range(blocks):
                part, slot = rim_slot(a, b, blocks)
                value = strip_columns(lane, packed[k, pl.ds(part * ROWS, ROWS), :], slot)
                to = pl.ds(pl.multiple_of(ROWS + source * strip_rows + b * ROWS, ROWS), ROWS)
                if a == 0:
                    logf[2, to, :] = value
                else:
                    given[a - 1, 2, to, :] = value

    def fields(i, carry):
        rows = pl.ds(pl.multiple_of(i * ROWS, ROWS), ROWS)
        for t in range(3):
            fric[t, rows, :] = jnp.exp(logf[t, rows, :])
            for c in range(2):
                force[c, t, rows, :] = given[2 + c, t, rows, :] * (given[c, t, rows, :] - surf[c, t, rows, :])
        return carry

    lax.fori_loop(0, FRAME // ROWS, fields, 0, unroll=True)
    coefficients(coef, visc, fric, ice, lane)
    old, new = state, other
    for _ in range(SWEEPS):
        for l in range(LAYERS):
            sweep_layer(coef, old, new, l, lane, force if l == LAYERS - 1 else None)
        old, new = new, old
    outs = []
    for t in range(2):
        copy = pltpu.make_async_copy(old.at[:, t, main, :], out.at[:, :, pl.ds(t * LANES, LANES)], sems.at[t])
        copy.start()
        outs.append(copy)

    def finish(i, carry):
        r = pl.multiple_of(i * ROWS, ROWS)
        rows, east, west = pl.ds(r + ROWS, ROWS), pl.ds(r + ROWS + 1, ROWS), pl.ds(r + ROWS - 1, ROWS)
        centre = [logf[t, rows, :] for t in range(3)]
        north, south = after(centre, lane), before(centre, lane)
        row = lax.broadcasted_iota(jnp.int32, (ROWS, LANES), 0) + r
        in_west = jnp.logical_or(row != 0, mx != 0)
        in_east = jnp.logical_or(row != TILE - 1, mx != size_x - 1)
        in_south = jnp.logical_or(lane != 0, me != 0)
        in_north = jnp.logical_or(lane != LANES - 1, me != n - 1)
        for t in range(2):
            c = centre[t]
            smooth = jnp.where(in_west, c - logf[t, west, :], 0.0) + jnp.where(in_east, c - logf[t, east, :], 0.0)
            below_ = c - south[t]
            above_ = c - north[t]
            smooth = smooth + (jnp.where(in_south, below_, 0.0) if t == 0 else below_)
            smooth = smooth + (jnp.where(in_north, above_, 0.0) if t == 1 else above_)
            inner = pl.ds(r, ROWS)
            basal = fric[t, rows, :] * (
                bed[0, t, inner, :] * old[0, t, rows, :] + bed[1, t, inner, :] * old[LAYERS, t, rows, :]
            )
            grad[t, inner, :] = basal + TIKHONOV * smooth
        return carry

    lax.fori_loop(0, BLOCKS, finish, 0, unroll=8)
    for k in range(n):
        to = lax.rem(me + k, n)
        rows = pl.ds(pl.multiple_of(to * strip_rows, ROWS), strip_rows)
        copy = pltpu.make_async_copy(grad.at[:, rows, :], grads[k], sems.at[2 + k])
        copy.start()
        outs.append(copy)
    for copy in outs:
        copy.wait()


def unpack_gradient(n, *refs):
    parts, out = refs[:n], refs[n]
    me = lax.axis_index("gy")
    for k in range(n):
        source = lax.rem(me - k + n, n)
        for t in range(2):
            out[:, pl.ds(pl.multiple_of(source * TILE + t * LANES, LANES), LANES)] = parts[k][t]


def f32(*shape):
    return jax.ShapeDtypeStruct(shape, jnp.float32)


def per_device(
    adjoint_start,
    viscosity,
    base_velocity,
    surface_velocity,
    ice_mask,
    log_friction,
    observed_velocity,
    obs_weight,
):
    n = lax.axis_size("gy")
    size_x = lax.axis_size("gx")
    strip_rows = log_friction.shape[0]
    vmem = pl.BlockSpec(memory_space=pltpu.VMEM)
    smem = pl.BlockSpec(memory_space=pltpu.SMEM)
    anywhere = pl.BlockSpec(memory_space=pl.ANY)
    params = pltpu.CompilerParams(vmem_limit_bytes=VMEM_BYTES)
    adjoint = adjoint_start.reshape((2 * LAYERS, TILE, TILE))

    def ring(k):
        return [(i, (i + k) % n) for i in range(n)]

    def line(size, k):
        return [(i, i + k) for i in range(size) if 0 <= i + k < size]

    packed = pl.pallas_call(
        functools.partial(pack_strips, n, strip_rows),
        out_shape=[f32(control_rows(strip_rows), LANES)] * n + [f32(4, 2, strip_rows, LANES)] * n,
        in_specs=[vmem] * 3,
        out_specs=[vmem] * (2 * n),
        compiler_params=params,
    )(log_friction, observed_velocity, obs_weight)
    controls, datas = packed[:n], packed[n:]
    controls = [controls[0]] + [lax.ppermute(controls[k], "gy", ring(k)) for k in range(1, n)]
    datas = [datas[0]] + [lax.ppermute(datas[k], "gy", ring(k)) for k in range(1, n)]

    columns_up, columns_down = pl.pallas_call(
        pack_columns,
        out_shape=[f32(HALF, LANES)] * 2,
        in_specs=[smem, vmem, vmem, vmem],
        out_specs=[vmem] * 2,
        compiler_params=params,
    )(ice_mask, adjoint, viscosity, surface_velocity)
    from_left = lax.ppermute(columns_up, "gy", line(n, 1))
    from_right = lax.ppermute(columns_down, "gy", line(n, -1))

    rows_up, rows_down = pl.pallas_call(
        functools.partial(pack_rows, n, strip_rows),
        out_shape=[f32(RIM_FIELDS, 3, ROWS, LANES)] * 2,
        in_specs=[smem] + [vmem] * (5 + n),
        out_specs=[vmem] * 2,
        compiler_params=params,
    )(ice_mask, adjoint, viscosity, surface_velocity, from_left, from_right, *controls)
    above = lax.ppermute(rows_up, "gx", line(size_x, 1))
    below = lax.ppermute(rows_down, "gx", line(size_x, -1))

    def frames(*leading):
        return pltpu.VMEM(leading + (3, FRAME, LANES), jnp.float32)

    *grads, out = pl.pallas_call(
        functools.partial(sweeps_kernel, n, strip_rows),
        out_shape=[f32(2, strip_rows, LANES)] * n + [f32(2 * LAYERS, TILE, TILE)],
        in_specs=[smem] + [anywhere] * 4 + [vmem] * 2 + [anywhere] * (2 + 2 * n),
        out_specs=[anywhere] * (n + 1),
        scratch_shapes=[
            frames(8),
            frames(8),
            frames(4),
            frames(2),
            frames(),
            frames(),
            frames(),
            frames(4),
            pltpu.VMEM((2, 2, TILE, LANES), jnp.float32),
            frames(LAYERS, 9),
            frames(2),
            pltpu.VMEM((2, TILE, LANES), jnp.float32),
            pltpu.VMEM((n, ROWS * rim_tiles(strip_rows), LANES), jnp.float32),
            pltpu.SemaphoreType.DMA((20 + 4 * n,)),
        ],
        compiler_params=params,
    )(
        ice_mask,
        adjoint,
        viscosity,
        surface_velocity,
        base_velocity,
        from_left,
        from_right,
        above,
        below,
        *controls,
        *datas,
    )
    parts = [grads[0]] + [lax.ppermute(grads[k], "gy", ring(k)) for k in range(1, n)]
    gradient = pl.pallas_call(
        functools.partial(unpack_gradient, n),
        out_shape=f32(strip_rows, n * TILE),
        in_specs=[vmem] * n,
        out_specs=vmem,
        compiler_params=params,
    )(*parts)
    return gradient, out.reshape(adjoint_start.shape)


def solution(mesh):
    placed = (
        P(None, None, "gx", "gy"),
        P(None, "gx", "gy"),
        P(None, "gx", "gy"),
        P(None, "gx", "gy"),
        P("gx", "gy"),
        P(("gx", "gy"), None),
        P(None, ("gx", "gy"), None),
        P(None, ("gx", "gy"), None),
    )
    return jax.shard_map(
        per_device,
        mesh=mesh,
        in_specs=placed,
        out_specs=(P(("gx", "gy"), None), P(None, None, "gx", "gy")),
        check_vma=False,
    )
```

```python
import functools

import jax
import jax.numpy as jnp
from jax import lax
from jax.experimental import pallas as pl
from jax.experimental.pallas import tpu as pltpu
from jax.sharding import PartitionSpec as P

SWEEPS = 4
DAMPING = 0.8
VERTICAL = 2.0
COUPLING = 3.0
TIKHONOV = 0.25

LAYERS = 4
LANES = 128
ROWS = 8
TILE = 256
FRAME = TILE + 2 * ROWS
HALF = TILE // 2
BLOCKS = TILE // ROWS
FIRST = 4
STEPS = BLOCKS + 1
TILE_FIELDS = 15
RIM_FIELDS = 20
PAIRS = RIM_FIELDS // 2
EDGE_ROWS = 4 * ROWS
MIB = 1024 * 1024


def row_index():
    return lax.broadcasted_iota(jnp.int32, (ROWS, LANES), 0)


def lane_index():
    return lax.broadcasted_iota(jnp.int32, (ROWS, LANES), 1)


def roll_to(x, shift):
    shift = shift % LANES
    return x if shift == 0 else pltpu.roll(x, shift, 1)


def after(x, lane):
    a, b, c = (roll_to(v, -1) for v in x)
    last = lane == LANES - 1
    return jnp.where(last, b, a), jnp.where(last, c, b), jnp.where(last, a, c)


def before(x, lane):
    a, b, c = (roll_to(v, 1) for v in x)
    first = lane == 0
    return jnp.where(first, c, a), jnp.where(first, a, b), jnp.where(first, b, c)


def rim_slot(array, block, strip_blocks):
    position = array * strip_blocks + block
    return position // 16, position % 16


def rim_tiles(strip_rows):
    return -(-5 * (strip_rows // ROWS) // 16)


def control_rows(strip_rows):
    return 2 * strip_rows + EDGE_ROWS + ROWS * rim_tiles(strip_rows)


def pack_strips(n, strip_rows, logf, obs, weight, controls, datas):
    me = lax.axis_index("gy")
    lane = lane_index()
    blocks = strip_rows // ROWS
    edge = pl.multiple_of(jnp.where(me == 0, 0, strip_rows - ROWS), ROWS)
    own = (row_index() < 4) == (me == 0)
    strips = [logf.at[...], obs.at[0], obs.at[1], weight.at[0], weight.at[1]]
    width = n * TILE
    for k in range(n):
        to = lax.rem(me + k, n)
        column = pl.multiple_of(to * TILE, TILE)
        left = pl.multiple_of(jnp.maximum(column - LANES, 0), LANES)
        right = pl.multiple_of(jnp.minimum(column + TILE, width - LANES), LANES)
        control, data = controls[k], datas[k]
        for t in range(2):
            columns = pl.ds(column + t * LANES, LANES)
            control[pl.ds(t * strip_rows, strip_rows), :] = logf[:, columns]
            for a in range(4):
                data[a, t] = strips[a + 1][:, columns]
            for a in range(2):
                ends = [strips[a + i][pl.ds(edge, ROWS), columns] for i in (1, 3)]
                both = jnp.where(own, ends[0], pltpu.roll(ends[1], 4, 0))
                control[pl.ds(2 * strip_rows + (a * 2 + t) * ROWS, ROWS), :] = both
        packed = [jnp.zeros((ROWS, LANES), jnp.float32) for _ in range(rim_tiles(strip_rows))]
        for a in range(5):
            for b in range(blocks):
                part, slot = rim_slot(a, b, blocks)
                rows = pl.ds(b * ROWS, ROWS)
                both = jnp.where(lane < 64, strips[a][rows, pl.ds(right, LANES)], strips[a][rows, pl.ds(left, LANES)])
                packed[part] = jnp.where(lane // 8 == slot, roll_to(both, 8 * slot + 4), packed[part])
        for part, value in enumerate(packed):
            control[pl.ds(2 * strip_rows + EDGE_ROWS + part * ROWS, ROWS), :] = value


def tile_field(a, adjoint, viscosity, surface):
    if a < 8:
        return adjoint.at[a]
    if a < 12:
        return viscosity.at[a - 8]
    return surface.at[a - 12]


def pack_columns(mask, adjoint, viscosity, surface, up, down, first):
    lane = lane_index()

    def step(r, carry):
        to_up = jnp.zeros((ROWS, LANES), jnp.float32)
        to_down = jnp.zeros((ROWS, LANES), jnp.float32)
        for h in range(2):
            rows = pl.ds(pl.multiple_of(h * HALF + r * ROWS, ROWS), ROWS)
            for a in range(TILE_FIELDS):
                slot = h * TILE_FIELDS + a
                here = lane // 4 == slot
                if a == TILE_FIELDS - 1:
                    low = mask[h, 0].astype(jnp.float32)
                    high = mask[h, 1].astype(jnp.float32)
                    to_up = jnp.where(here, high, to_up)
                    to_down = jnp.where(here, low, to_down)
                else:
                    field = tile_field(a, adjoint, viscosity, surface)
                    to_up = jnp.where(here, roll_to(field[rows, LANES:], 4 * slot + 4), to_up)
                    to_down = jnp.where(here, roll_to(field[rows, :LANES], 4 * slot), to_down)
        rows = pl.ds(pl.multiple_of(first + r * ROWS, ROWS), ROWS)
        up[rows, :] = to_up
        down[rows, :] = to_down
        return carry

    lax.fori_loop(0, HALF // ROWS, step, 0, unroll=4)


def start_copies(sems, pairs):
    copies = [pltpu.make_async_copy(source, target, sems.at[i]) for i, (source, target) in enumerate(pairs)]
    for copy in copies:
        copy.start()
    return copies


def pack_kernel(n, strip_rows, mask, logf, obs, weight, adjoint, viscosity, surface, *rest):
    controls, datas = rest[:n], rest[n : 2 * n]
    logf_in, obs_in, weight_in, adjoint_in, viscosity_in, surface_in, sems = rest[2 * n :]
    copies = start_copies(
        sems,
        [
            (logf, logf_in),
            (obs, obs_in),
            (weight, weight_in),
            (adjoint, adjoint_in),
            (viscosity, viscosity_in),
            (surface, surface_in),
        ],
    )
    for copy in copies[:3]:
        copy.wait()
    pack_strips(n, strip_rows, logf_in, obs_in, weight_in, controls, datas)
    for copy in copies[3:]:
        copy.wait()
    pack_columns(
        mask, adjoint_in, viscosity_in, surface_in, controls[1], controls[n - 1], control_rows(strip_rows)
    )


def side_columns(lane, from_left, from_right, slot):
    left = roll_to(from_left, -(4 * slot + 4))
    right = roll_to(from_right, -4 * slot)
    return jnp.where(lane < 4, right, jnp.where(lane >= LANES - 4, left, 0.0))


def strip_columns(lane, packed, slot):
    value = roll_to(packed, -(8 * slot + 4))
    return jnp.where(jnp.logical_or(lane < 4, lane >= LANES - 4), value, 0.0)


def sides_at(n, strip_rows, controls, row):
    me = lax.axis_index("gy")
    rows = pl.ds(pl.multiple_of(control_rows(strip_rows) + row, ROWS), ROWS)
    left = jnp.where(me > 0, controls[1][rows, :], 0.0)
    right = jnp.where(me < n - 1, controls[n - 1][rows, :], 0.0)
    return left, right


def pack_rows(n, strip_rows, mask, adjoint, viscosity, surface, *rest):
    controls, (up, down, adjoint_in, viscosity_in, surface_in, rim, sems) = rest[:n], rest[n:]
    me = lax.axis_index("gy")
    lane, sub = lane_index(), row_index()
    blocks = strip_rows // ROWS
    copies = []
    for h, row in ((0, 0), (1, TILE - ROWS)):
        rows = pl.ds(row, ROWS)
        copies += [
            (adjoint.at[:, rows, :], adjoint_in.at[h]),
            (viscosity.at[:, rows, :], viscosity_in.at[h]),
            (surface.at[:, rows, :], surface_in.at[h]),
        ]
    copies = start_copies(sems, copies)
    for h, owner in ((1, n - 1), (0, 0)):
        block = blocks - 1 if h else 0
        for k in range(n):

            @pl.when(lax.rem(me - k + n, n) == owner)
            def _():
                control = controls[k]
                for a in range(5):
                    for t in range(2):
                        if a == 0:
                            rim[h, a, t] = control[pl.ds(t * strip_rows + block * ROWS, ROWS), :]
                            continue
                        both = control[pl.ds(2 * strip_rows + ((a - 1) % 2 * 2 + t) * ROWS, ROWS), :]
                        rim[h, a, t] = both if a < 3 else pltpu.roll(both, 4, 0)
                    part, slot = rim_slot(a, block, blocks)
                    packed = control[pl.ds(2 * strip_rows + EDGE_ROWS + part * ROWS, ROWS), :]
                    rim[h, a, 2] = strip_columns(lane, packed, slot)

    for copy in copies:
        copy.wait()
    for message, h in ((up, 1), (down, 0)):
        left, right = sides_at(n, strip_rows, controls, h * (HALF - ROWS))

        def field(a, t):
            if a >= TILE_FIELDS:
                return rim[h, a - TILE_FIELDS, t]
            if t == 2:
                return side_columns(lane, left, right, h * TILE_FIELDS + a)
            if a == TILE_FIELDS - 1:
                return jnp.full((ROWS, LANES), mask[h, t].astype(jnp.float32))
            return tile_field(a, adjoint_in.at[h], viscosity_in.at[h], surface_in.at[h])[:, t * LANES : (t + 1) * LANES]

        own = sub >= 4 if h else sub < 4
        for a in range(PAIRS):
            for t in range(3):
                message[a, t] = jnp.where(own, field(a, t), pltpu.roll(field(a + PAIRS, t), 4, 0))


def rim_rows(message, a, t):
    if a < PAIRS:
        return message[a, t]
    return pltpu.roll(message[a - PAIRS, t], 4, 0)


E_, N_, S_, U_, V_, K0_, K1_, I0_, I1_ = range(9)


def coefficients(coef, visc, ice, lane, fric=None):
    def step(i, carry):
        r = FIRST + i * ROWS
        rows, east, west = pl.ds(r, ROWS), pl.ds(r + 1, ROWS), pl.ds(r - 1, ROWS)
        cells = [ice[t, rows, :] for t in range(3)]
        layers = [[visc[l, t, rows, :] for t in range(3)] for l in range(LAYERS)]
        for l in range(LAYERS):
            centre = layers[l]
            if l == 0 and fric is None:
                for t in range(3):
                    coef[l, U_, t, rows, :] = (0.5 * VERTICAL) * (centre[t] + layers[l + 1][t])
                continue
            north, south = after(centre, lane), before(centre, lane)
            for t in range(3):
                c = centre[t]
                e = 0.5 * (c + visc[l, t, east, :])
                w = 0.5 * (c + visc[l, t, west, :])
                nf = 0.5 * (c + north[t])
                sf = 0.5 * (c + south[t])
                coef[l, E_, t, rows, :] = e
                coef[l, N_, t, rows, :] = nf
                coef[l, S_, t, rows, :] = sf
                vertical = None
                if l < LAYERS - 1:
                    u = (0.5 * VERTICAL) * (c + layers[l + 1][t])
                    coef[l, U_, t, rows, :] = u
                    vertical = u
                if l > 0:
                    lower = (0.5 * VERTICAL) * (c + layers[l - 1][t])
                    vertical = lower if vertical is None else vertical + lower
                if l == 0:
                    vertical = vertical + fric[t, rows, :]
                coef[l, V_, t, rows, :] = (0.25 * COUPLING) * c
                rest = COUPLING * c + (1.0 - cells[t])
                ew, ns = e + w, nf + sf
                for c_, ax, ay in ((0, 4.0, 1.0), (1, 1.0, 4.0)):
                    own = (ax * ew if ax != 1.0 else ew) + (ay * ns if ay != 1.0 else ns) + vertical
                    inverse = DAMPING * cells[t] / (own + rest)
                    coef[l, I0_ + c_, t, rows, :] = inverse
                    coef[l, K0_ + c_, t, rows, :] = cells[t] - own * inverse
        return carry

    lax.fori_loop(0, STEPS, step, 0, unroll=STEPS)


def sweep_layer(coef, old, new, l, lane, force=None, last=False):
    first, steps, tiles = (ROWS, BLOCKS, 2) if last else (FIRST, STEPS, 3)

    def step(i, carry):
        r = first + i * ROWS
        rows, east, west = pl.ds(r, ROWS), pl.ds(r + 1, ROWS), pl.ds(r - 1, ROWS)
        e = [coef[l, E_, t, rows, :] for t in range(tiles)]
        w = [coef[l, E_, t, west, :] for t in range(tiles)]
        fluxes, mixes = [], []
        for c in range(2):
            m = [old[c * LAYERS + l, t, rows, :] for t in range(3)]
            me = [old[c * LAYERS + l, t, east, :] for t in range(3)]
            mw = [old[c * LAYERS + l, t, west, :] for t in range(3)]
            mn, ms = after(m, lane), before(m, lane)
            across = [me[t] - mw[t] for t in range(3)]
            an, as_ = after(across, lane), before(across, lane)
            mixes.append([an[t] - as_[t] for t in range(tiles)])
            flux = []
            for t in range(tiles):
                x = e[t] * me[t] + w[t] * mw[t]
                y = coef[l, N_, t, rows, :] * mn[t] + coef[l, S_, t, rows, :] * ms[t]
                total = 4.0 * x + y if c == 0 else x + 4.0 * y
                if l < LAYERS - 1:
                    total = total + coef[l, U_, t, rows, :] * old[c * LAYERS + l + 1, t, rows, :]
                if l > 0:
                    total = total + coef[l - 1, U_, t, rows, :] * old[c * LAYERS + l - 1, t, rows, :]
                if force is not None:
                    total = total + force[c, t, rows, :]
                flux.append((total, m[t]))
            fluxes.append(flux)
        for c in range(2):
            for t in range(tiles):
                total, m = fluxes[c][t]
                total = total + coef[l, V_, t, rows, :] * mixes[1 - c][t]
                new[c * LAYERS + l, t, rows, :] = (
                    coef[l, K0_ + c, t, rows, :] * m + coef[l, I0_ + c, t, rows, :] * total
                )
        return carry

    lax.fori_loop(0, steps, step, 0, unroll=steps)


def before_forcing(n, strip_rows, mask, adjoint, viscosity, base, above, below, *rest):
    controls = rest[:n]
    terms, first, second, third, fourth, visc_out, ice_out = rest[n : n + 7]
    s0, s1, s2, s3, s4, visc, ice, logf, fric, bed, coef, terms_in, reach, packed, sems = rest[n + 7 :]
    me, mx = lax.axis_index("gy"), lax.axis_index("gx")
    size_x = lax.axis_size("gx")
    lane = lane_index()
    blocks = strip_rows // ROWS
    main = pl.ds(ROWS, TILE)
    pairs = []
    for t in range(2):
        columns = pl.ds(t * LANES, LANES)
        pairs += [
            (adjoint.at[:, :, columns], s0.at[:, t, main, :]),
            (viscosity.at[:, :, columns], visc.at[:, t, main, :]),
            (base.at[:, :, columns], bed.at[:, t]),
        ]
    for k in range(n):
        source = lax.rem(me - k + n, n)
        rows = pl.ds(pl.multiple_of(ROWS + source * strip_rows, ROWS), strip_rows)
        tail = pl.ds(2 * strip_rows + EDGE_ROWS, ROWS * rim_tiles(strip_rows))
        pairs += [
            (controls[k].at[0:strip_rows], logf.at[0, rows, :]),
            (controls[k].at[strip_rows : 2 * strip_rows], logf.at[1, rows, :]),
            (controls[k].at[tail], packed.at[k]),
        ]
    copies = start_copies(sems, pairs)

    for h in range(2):
        for t in range(2):
            ice[t, pl.ds(ROWS + h * HALF, HALF), :] = jnp.full((HALF, LANES), mask[h, t].astype(jnp.float32))
    for message, row in ((above, 0), (below, ROWS + TILE)):
        rows = pl.ds(row, ROWS)
        for t in range(3):
            for a in range(8):
                s0[a, t, rows, :] = rim_rows(message, a, t)
            for a in range(4):
                visc[a, t, rows, :] = rim_rows(message, 8 + a, t)
            ice[t, rows, :] = rim_rows(message, 14, t)
            logf[t, rows, :] = rim_rows(message, 15, t)

    def sides(r, carry):
        left, right = sides_at(n, strip_rows, controls, r * ROWS)
        for h in range(2):
            to = pl.ds(pl.multiple_of(ROWS + h * HALF + r * ROWS, ROWS), ROWS)
            for a in range(TILE_FIELDS):
                slot = h * TILE_FIELDS + a
                if a < 8:
                    s0[a, 2, to, :] = side_columns(lane, left, right, slot)
                elif a < 12:
                    visc[a - 8, 2, to, :] = side_columns(lane, left, right, slot)
                elif a == 14:
                    ice[2, to, :] = side_columns(lane, left, right, slot)
        return carry

    lax.fori_loop(0, HALF // ROWS, sides, 0, unroll=4)
    for copy in copies:
        copy.wait()
    for k in range(n):
        source = lax.rem(me - k + n, n)
        for b in range(blocks):
            part, slot = rim_slot(0, b, blocks)
            to = pl.ds(pl.multiple_of(ROWS + source * strip_rows + b * ROWS, ROWS), ROWS)
            logf[2, to, :] = strip_columns(lane, packed[k, pl.ds(part * ROWS, ROWS), :], slot)
    for i in range(FRAME // ROWS):
        rows = pl.ds(i * ROWS, ROWS)
        for t in range(3):
            fric[t, rows, :] = jnp.exp(logf[t, rows, :])
    coefficients(coef, visc, ice, lane, fric)

    outs = [(visc, visc_out), (ice, ice_out)]
    for l in range(LAYERS):
        sweep_layer(coef, s0, s1, l, lane)
    outs += [(s1.at[pl.ds(c * LAYERS + 2, 2)], first.at[c]) for c in range(2)]
    for l in range(3):
        sweep_layer(coef, s1, s2, l, lane)
    outs += [(s2.at[pl.ds(c * LAYERS + 1, 2)], second.at[c]) for c in range(2)]
    for l in range(2):
        sweep_layer(coef, s2, s3, l, lane)
    outs += [(s3.at[pl.ds(c * LAYERS, 2)], third.at[c]) for c in range(2)]
    copies = start_copies(sems, outs)
    sweep_layer(coef, s3, s4, 0, lane, last=True)

    def finish(i, carry):
        r = pl.multiple_of(i * ROWS, ROWS)
        rows, east, west = pl.ds(r + ROWS, ROWS), pl.ds(r + ROWS + 1, ROWS), pl.ds(r + ROWS - 1, ROWS)
        centre = [logf[t, rows, :] for t in range(3)]
        north, south = after(centre, lane), before(centre, lane)
        row = row_index() + r
        in_west = jnp.logical_or(row != 0, mx != 0)
        in_east = jnp.logical_or(row != TILE - 1, mx != size_x - 1)
        in_south = jnp.logical_or(lane != 0, me != 0)
        in_north = jnp.logical_or(lane != LANES - 1, me != n - 1)
        inner = pl.ds(r, ROWS)
        for t in range(2):
            c = centre[t]
            smooth = jnp.where(in_west, c - logf[t, west, :], 0.0) + jnp.where(in_east, c - logf[t, east, :], 0.0)
            left, right = c - south[t], c - north[t]
            smooth = smooth + (jnp.where(in_south, left, 0.0) if t == 0 else left)
            smooth = smooth + (jnp.where(in_north, right, 0.0) if t == 1 else right)
            total = TIKHONOV * smooth
            for component in range(2):
                along = coef[LAYERS - 1, I0_ + component, t, rows, :]
                for l in (2, 1, 0):
                    along = along * (coef[l, I0_ + component, t, rows, :] * coef[l, U_, t, rows, :])
                reach[component, t, inner, :] = along
                weight = fric[t, rows, :] * bed[component, t, inner, :]
                total = total + weight * s4[component * LAYERS, t, rows, :]
                terms_in[1 + component, t, inner, :] = weight * along
            terms_in[0, t, inner, :] = total
        return carry

    lax.fori_loop(0, BLOCKS, finish, 0, unroll=8)
    used = len(copies)
    more = [(terms_in, terms), (reach, fourth.at[1])]
    more += [(s4.at[c * LAYERS, pl.ds(0, 2), main, :], fourth.at[0, c]) for c in range(2)]
    for copy in copies + start_copies(sems.at[pl.ds(used, len(more))], more):
        copy.wait()


def gradient_kernel(n, strip_rows, terms, surface, *rest):
    datas, grads = rest[:n], rest[n:]
    me = lax.axis_index("gy")
    for k in range(n):
        source = lax.rem(me - k + n, n)
        for b in range(strip_rows // ROWS):
            rows = pl.ds(pl.multiple_of(source * strip_rows + b * ROWS, ROWS), ROWS)
            part = pl.ds(b * ROWS, ROWS)
            for t in range(2):
                total = terms[0, t, rows, :]
                for c in range(2):
                    force = datas[k][2 + c, t, part, :] * (
                        datas[k][c, t, part, :] - surface[c, rows, t * LANES : (t + 1) * LANES]
                    )
                    total = total + terms[1 + c, t, rows, :] * force
                grads[k][t, part, :] = total


def after_forcing(n, strip_rows, surface, above, below, first, second, third, fourth, visc_in, ice_in, *rest):
    controls, datas, out = rest[:n], rest[n : 2 * n], rest[2 * n]
    s1, s2, s3, s4, visc, ice, bottom, surf, given, coef, force, packed, sems = rest[2 * n + 1 :]
    me = lax.axis_index("gy")
    lane = lane_index()
    blocks = strip_rows // ROWS
    main = pl.ds(ROWS, TILE)
    pairs = [(visc_in, visc), (ice_in, ice)]
    for t in range(2):
        pairs += [(surface.at[:, :, pl.ds(t * LANES, LANES)], surf.at[:, t, main, :])]
    for k in range(n):
        source = lax.rem(me - k + n, n)
        rows = pl.ds(pl.multiple_of(ROWS + source * strip_rows, ROWS), strip_rows)
        tail = pl.ds(2 * strip_rows + EDGE_ROWS, ROWS * rim_tiles(strip_rows))
        pairs += [(datas[k], given.at[:, 0:2, rows, :]), (controls[k].at[tail], packed.at[k])]
    early = len(pairs)
    pairs += [(first.at[c], s1.at[pl.ds(c * LAYERS + 2, 2)]) for c in range(2)]
    pairs += [(second.at[c], s2.at[pl.ds(c * LAYERS + 1, 2)]) for c in range(2)]
    pairs += [(third.at[c], s3.at[pl.ds(c * LAYERS, 2)]) for c in range(2)]
    pairs += [(fourth, bottom)]
    copies = start_copies(sems, pairs)
    for message, row in ((above, 0), (below, ROWS + TILE)):
        rows = pl.ds(row, ROWS)
        for t in range(3):
            for c in range(2):
                surf[c, t, rows, :] = rim_rows(message, 12 + c, t)
            for a in range(4):
                given[a, t, rows, :] = rim_rows(message, 16 + a, t)

    def sides(r, carry):
        left, right = sides_at(n, strip_rows, controls, r * ROWS)
        for h in range(2):
            to = pl.ds(pl.multiple_of(ROWS + h * HALF + r * ROWS, ROWS), ROWS)
            for c in range(2):
                surf[c, 2, to, :] = side_columns(lane, left, right, h * TILE_FIELDS + 12 + c)
        return carry

    lax.fori_loop(0, HALF // ROWS, sides, 0, unroll=4)
    for copy in copies[:early]:
        copy.wait()
    for k in range(n):
        source = lax.rem(me - k + n, n)
        for a in range(1, 5):
            for b in range(blocks):
                part, slot = rim_slot(a, b, blocks)
                to = pl.ds(pl.multiple_of(ROWS + source * strip_rows + b * ROWS, ROWS), ROWS)
                given[a - 1, 2, to, :] = strip_columns(lane, packed[k, pl.ds(part * ROWS, ROWS), :], slot)
    coefficients(coef, visc, ice, lane)
    for copy in copies[early:]:
        copy.wait()

    def add_forcing(i, carry):
        rows = pl.ds(FIRST + i * ROWS, ROWS)
        for t in range(3):
            for c in range(2):
                value = given[2 + c, t, rows, :] * (given[c, t, rows, :] - surf[c, t, rows, :])
                force[c, t, rows, :] = value
                value = coef[3, I0_ + c, t, rows, :] * value
                s1[c * LAYERS + 3, t, rows, :] = s1[c * LAYERS + 3, t, rows, :] + value
                value = coef[2, I0_ + c, t, rows, :] * (coef[2, U_, t, rows, :] * value)
                s2[c * LAYERS + 2, t, rows, :] = s2[c * LAYERS + 2, t, rows, :] + value
                value = coef[1, I0_ + c, t, rows, :] * (coef[1, U_, t, rows, :] * value)
                s3[c * LAYERS + 1, t, rows, :] = s3[c * LAYERS + 1, t, rows, :] + value
        return carry

    lax.fori_loop(0, STEPS, add_forcing, 0, unroll=11)
    for i in range(BLOCKS):
        rows, inner = pl.ds(ROWS + i * ROWS, ROWS), pl.ds(i * ROWS, ROWS)
        for t in range(2):
            for c in range(2):
                s4[c * LAYERS, t, rows, :] = bottom[0, c, t, inner, :] + bottom[1, c, t, inner, :] * force[c, t, rows, :]
    sweep_layer(coef, s1, s2, 3, lane, force)
    sweep_layer(coef, s2, s3, 2, lane)
    sweep_layer(coef, s2, s3, 3, lane, force)
    for l in (1, 2, 3):
        sweep_layer(coef, s3, s4, l, lane, force if l == 3 else None, last=True)
    outs = [(s4.at[:, t, main, :], out.at[:, :, pl.ds(t * LANES, LANES)]) for t in range(2)]
    for copy in start_copies(sems, outs):
        copy.wait()


def unpack_gradient(n, *refs):
    parts, out = refs[:n], refs[n]
    me = lax.axis_index("gy")
    for k in range(n):
        source = lax.rem(me + k, n)
        for t in range(2):
            out[:, pl.ds(pl.multiple_of(source * TILE + t * LANES, LANES), LANES)] = parts[k][t]


def f32(*shape):
    return jax.ShapeDtypeStruct(shape, jnp.float32)


def vmem_f32(*shape):
    return pltpu.VMEM(shape, jnp.float32)


def frames(*leading):
    return vmem_f32(*leading, 3, FRAME, LANES)


def f32_frames(*leading):
    return f32(*leading, 3, FRAME, LANES)


def per_device(
    adjoint_start,
    viscosity,
    base_velocity,
    surface_velocity,
    ice_mask,
    log_friction,
    observed_velocity,
    obs_weight,
):
    n = lax.axis_size("gy")
    size_x = lax.axis_size("gx")
    strip_rows = log_friction.shape[0]
    width = n * TILE
    vmem = pl.BlockSpec(memory_space=pltpu.VMEM)
    smem = pl.BlockSpec(memory_space=pltpu.SMEM)
    anywhere = pl.BlockSpec(memory_space=pl.ANY)
    adjoint = adjoint_start.reshape((2 * LAYERS, TILE, TILE))
    rim_size = ROWS * rim_tiles(strip_rows)

    def params(mib):
        return pltpu.CompilerParams(vmem_limit_bytes=mib * MIB)

    def ring(k):
        return [(i, (i + k) % n) for i in range(n)]

    def line(size, k):
        return [(i, i + k) for i in range(size) if 0 <= i + k < size]

    def control_shape(k):
        return f32(control_rows(strip_rows) + (HALF if k in (1, n - 1) else 0), LANES)

    packed = pl.pallas_call(
        functools.partial(pack_kernel, n, strip_rows),
        out_shape=[control_shape(k) for k in range(n)] + [f32(4, 2, strip_rows, LANES)] * n,
        in_specs=[smem] + [anywhere] * 6,
        out_specs=[vmem] * (2 * n),
        scratch_shapes=[
            vmem_f32(strip_rows, width),
            vmem_f32(2, strip_rows, width),
            vmem_f32(2, strip_rows, width),
            vmem_f32(2 * LAYERS, TILE, TILE),
            vmem_f32(LAYERS, TILE, TILE),
            vmem_f32(2, TILE, TILE),
            pltpu.SemaphoreType.DMA((6,)),
        ],
        compiler_params=params(56),
    )(ice_mask, log_friction, observed_velocity, obs_weight, adjoint, viscosity, surface_velocity)
    controls, datas = packed[:n], packed[n:]
    controls = [controls[0]] + [lax.ppermute(controls[k], "gy", ring(k)) for k in range(1, n)]
    controls, datas = lax.optimization_barrier((controls, datas))
    datas = [datas[0]] + [lax.ppermute(datas[k], "gy", ring(k)) for k in range(1, n)]

    rows_up, rows_down = pl.pallas_call(
        functools.partial(pack_rows, n, strip_rows),
        out_shape=[f32(PAIRS, 3, ROWS, LANES)] * 2,
        in_specs=[smem] + [anywhere] * 3 + [vmem] * n,
        out_specs=[vmem] * 2,
        scratch_shapes=[
            vmem_f32(2, 2 * LAYERS, ROWS, TILE),
            vmem_f32(2, LAYERS, ROWS, TILE),
            vmem_f32(2, 2, ROWS, TILE),
            vmem_f32(2, 5, 3, ROWS, LANES),
            pltpu.SemaphoreType.DMA((6,)),
        ],
        compiler_params=params(4),
    )(ice_mask, adjoint, viscosity, surface_velocity, *controls)
    above = lax.ppermute(rows_up, "gx", line(size_x, 1))
    below = lax.ppermute(rows_down, "gx", line(size_x, -1))

    terms, first, second, third, fourth, visc, ice = pl.pallas_call(
        functools.partial(before_forcing, n, strip_rows),
        out_shape=[
            f32(3, 2, TILE, LANES),
            f32_frames(2, 2),
            f32_frames(2, 2),
            f32_frames(2, 2),
            f32(2, 2, 2, TILE, LANES),
            f32_frames(LAYERS),
            f32_frames(),
        ],
        in_specs=[smem] + [anywhere] * 3 + [vmem] * (2 + n),
        out_specs=[anywhere] * 7,
        scratch_shapes=[frames(8)] * 5
        + [
            frames(LAYERS),
            frames(),
            frames(),
            frames(),
            vmem_f32(2, 2, TILE, LANES),
            frames(LAYERS, 9),
            vmem_f32(3, 2, TILE, LANES),
            vmem_f32(2, 2, TILE, LANES),
            vmem_f32(n, rim_size, LANES),
            pltpu.SemaphoreType.DMA((16 + 3 * n,)),
        ],
        compiler_params=params(42),
    )(ice_mask, adjoint, viscosity, base_velocity, above, below, *controls)

    grads = pl.pallas_call(
        functools.partial(gradient_kernel, n, strip_rows),
        out_shape=[f32(2, strip_rows, LANES)] * n,
        in_specs=[vmem] * (2 + n),
        out_specs=[vmem] * n,
        compiler_params=params(6),
    )(terms, surface_velocity, *datas)
    parts = [grads[0]] + [lax.ppermute(grads[k], "gy", ring(n - k)) for k in range(1, n)]

    out = pl.pallas_call(
        functools.partial(after_forcing, n, strip_rows),
        out_shape=f32(2 * LAYERS, TILE, TILE),
        in_specs=[anywhere] + [vmem] * 2 + [anywhere] * 6 + [vmem] * n + [anywhere] * n,
        out_specs=anywhere,
        scratch_shapes=[frames(8)] * 4
        + [
            frames(LAYERS),
            frames(),
            vmem_f32(2, 2, 2, TILE, LANES),
            frames(2),
            frames(4),
            frames(LAYERS, 9),
            frames(2),
            vmem_f32(n, rim_size, LANES),
            pltpu.SemaphoreType.DMA((12 + 2 * n,)),
        ],
        compiler_params=params(42),
    )(surface_velocity, above, below, first, second, third, fourth, visc, ice, *controls, *datas)

    gradient = pl.pallas_call(
        functools.partial(unpack_gradient, n),
        out_shape=f32(strip_rows, width),
        in_specs=[vmem] * n,
        out_specs=vmem,
        compiler_params=params(4),
    )(*parts)
    return gradient, out.reshape(adjoint_start.shape)


def solution(mesh):
    placed = (
        P(None, None, "gx", "gy"),
        P(None, "gx", "gy"),
        P(None, "gx", "gy"),
        P(None, "gx", "gy"),
        P("gx", "gy"),
        P(("gx", "gy"), None),
        P(None, ("gx", "gy"), None),
        P(None, ("gx", "gy"), None),
    )
    return jax.shard_map(
        per_device,
        mesh=mesh,
        in_specs=placed,
        out_specs=(P(("gx", "gy"), None), P(None, None, "gx", "gy")),
        check_vma=False,
    )
```

```python
import functools

import jax
import jax.numpy as jnp
from jax import lax
from jax.experimental import pallas as pl
from jax.experimental.pallas import tpu as pltpu
from jax.sharding import PartitionSpec as P

SWEEPS = 4
DAMPING = 0.8
VERTICAL = 2.0
COUPLING = 3.0
TIKHONOV = 0.25

LAYERS = 4
LANES = 128
ROWS = 8
TILE = 256
FRAME = TILE + 2 * ROWS
HALF = TILE // 2
BLOCKS = TILE // ROWS
FIRST = 4
STEPS = BLOCKS + 1
TILE_FIELDS = 15
RIM_FIELDS = 20
PAIRS = RIM_FIELDS // 2
EDGE_ROWS = 4 * ROWS
MIB = 1024 * 1024


def row_index():
    return lax.broadcasted_iota(jnp.int32, (ROWS, LANES), 0)


def lane_index():
    return lax.broadcasted_iota(jnp.int32, (ROWS, LANES), 1)


def roll_to(x, shift):
    shift = shift % LANES
    return x if shift == 0 else pltpu.roll(x, shift, 1)


def after(x, lane):
    a, b, c = (roll_to(v, -1) for v in x)
    last = lane == LANES - 1
    return jnp.where(last, b, a), jnp.where(last, c, b), jnp.where(last, a, c)


def before(x, lane):
    a, b, c = (roll_to(v, 1) for v in x)
    first = lane == 0
    return jnp.where(first, c, a), jnp.where(first, a, b), jnp.where(first, b, c)


def rim_slot(array, block, strip_blocks):
    position = array * strip_blocks + block
    return position // 16, position % 16


def rim_tiles(strip_rows):
    return -(-5 * (strip_rows // ROWS) // 16)


def control_rows(strip_rows):
    return 2 * strip_rows + EDGE_ROWS + ROWS * rim_tiles(strip_rows)


def pack_strips(n, strip_rows, logf, obs, weight, controls):
    me = lax.axis_index("gy")
    lane = lane_index()
    blocks = strip_rows // ROWS
    edge = pl.multiple_of(jnp.where(me == 0, 0, strip_rows - ROWS), ROWS)
    own = (row_index() < 4) == (me == 0)
    strips = [logf.at[...], obs.at[0], obs.at[1], weight.at[0], weight.at[1]]
    width = n * TILE
    for k in range(n):
        to = lax.rem(me + k, n)
        column = pl.multiple_of(to * TILE, TILE)
        left = pl.multiple_of(jnp.maximum(column - LANES, 0), LANES)
        right = pl.multiple_of(jnp.minimum(column + TILE, width - LANES), LANES)
        control = controls[k]
        for t in range(2):
            columns = pl.ds(column + t * LANES, LANES)
            control[pl.ds(t * strip_rows, strip_rows), :] = logf[:, columns]
            for a in range(2):
                ends = [strips[a + i][pl.ds(edge, ROWS), columns] for i in (1, 3)]
                both = jnp.where(own, ends[0], pltpu.roll(ends[1], 4, 0))
                control[pl.ds(2 * strip_rows + (a * 2 + t) * ROWS, ROWS), :] = both
        packed = [jnp.zeros((ROWS, LANES), jnp.float32) for _ in range(rim_tiles(strip_rows))]
        for a in range(5):
            for b in range(blocks):
                part, slot = rim_slot(a, b, blocks)
                rows = pl.ds(b * ROWS, ROWS)
                both = jnp.where(lane < 64, strips[a][rows, pl.ds(right, LANES)], strips[a][rows, pl.ds(left, LANES)])
                packed[part] = jnp.where(lane // 8 == slot, roll_to(both, 8 * slot + 4), packed[part])
        for part, value in enumerate(packed):
            control[pl.ds(2 * strip_rows + EDGE_ROWS + part * ROWS, ROWS), :] = value


def tile_field(a, state, visc, surf):
    if a < 8:
        return state.at[a]
    if a < 12:
        return visc.at[a - 8]
    return surf.at[a - 12]


CHUNKS = 2


def pack_columns(mask, state, visc, surf, up, down, first, chunk):
    lane = lane_index()
    count = HALF // ROWS // CHUNKS
    for r in range(chunk * count, (chunk + 1) * count):
        to_up = jnp.zeros((ROWS, LANES), jnp.float32)
        to_down = jnp.zeros((ROWS, LANES), jnp.float32)
        for h in range(2):
            rows = pl.ds(ROWS + h * HALF + r * ROWS, ROWS)
            for a in range(TILE_FIELDS):
                slot = h * TILE_FIELDS + a
                here = lane // 4 == slot
                if a == TILE_FIELDS - 1:
                    low = mask[h, 0].astype(jnp.float32)
                    high = mask[h, 1].astype(jnp.float32)
                    to_up = jnp.where(here, high, to_up)
                    to_down = jnp.where(here, low, to_down)
                else:
                    field = tile_field(a, state, visc, surf)
                    to_up = jnp.where(here, roll_to(field[1, rows, :], 4 * slot + 4), to_up)
                    to_down = jnp.where(here, roll_to(field[0, rows, :], 4 * slot), to_down)
        rows = pl.ds(first + r * ROWS, ROWS)
        up[rows, :] = to_up
        down[rows, :] = to_down


def start_copies(sems, pairs):
    copies = [pltpu.make_async_copy(source, target, sems.at[i]) for i, (source, target) in enumerate(pairs)]
    for copy in copies:
        copy.start()
    return copies


def pack_kernel(n, strip_rows, mask, logf, obs, weight, adjoint, viscosity, surface, *rest):
    controls, (state, visc, surf, logf_in, obs_in, weight_in, sems) = rest[:n], rest[n:]
    pairs = [(logf, logf_in), (obs, obs_in), (weight, weight_in)]
    size = HALF // CHUNKS
    for chunk in range(CHUNKS):
        for h in range(2):
            row = h * HALF + chunk * size
            for field, frame in ((adjoint, state), (viscosity, visc), (surface, surf)):
                for t in range(2):
                    source = field.at[:, pl.ds(row, size), pl.ds(t * LANES, LANES)]
                    pairs.append((source, frame.at[:, t, pl.ds(ROWS + row, size), :]))
    copies = start_copies(sems, pairs)
    for copy in copies[:3]:
        copy.wait()
    pack_strips(n, strip_rows, logf_in, obs_in, weight_in, controls)
    first = control_rows(strip_rows)
    for chunk in range(CHUNKS):
        for copy in copies[3 + 12 * chunk : 15 + 12 * chunk]:
            copy.wait()
        pack_columns(mask, state, visc, surf, controls[1], controls[n - 1], first, chunk)


def pack_observations(n, strip_rows, obs, weight, *rest):
    datas, (obs_in, weight_in, sems) = rest[:n], rest[n:]
    me = lax.axis_index("gy")
    for copy in start_copies(sems, [(obs, obs_in), (weight, weight_in)]):
        copy.wait()
    pairs = []
    for k in range(n):
        column = pl.multiple_of(lax.rem(me + k, n) * TILE, TILE)
        for t in range(2):
            columns = pl.ds(column + t * LANES, LANES)
            pairs.append((obs_in.at[:, :, columns], datas[k].at[0:2, t]))
            pairs.append((weight_in.at[:, :, columns], datas[k].at[2:4, t]))
    for copy in start_copies(sems, pairs):
        copy.wait()


def side_columns(lane, from_left, from_right, slot):
    left = roll_to(from_left, -(4 * slot + 4))
    right = roll_to(from_right, -4 * slot)
    return jnp.where(lane < 4, right, jnp.where(lane >= LANES - 4, left, 0.0))


def strip_columns(lane, packed, slot):
    value = roll_to(packed, -(8 * slot + 4))
    return jnp.where(jnp.logical_or(lane < 4, lane >= LANES - 4), value, 0.0)


def sides_at(n, strip_rows, controls, row):
    me = lax.axis_index("gy")
    rows = pl.ds(pl.multiple_of(control_rows(strip_rows) + row, ROWS), ROWS)
    left = jnp.where(me > 0, controls[1][rows, :], 0.0)
    right = jnp.where(me < n - 1, controls[n - 1][rows, :], 0.0)
    return left, right


def pack_rows(n, strip_rows, mask, state, visc, surf, *rest):
    controls, (up, down, rim) = rest[:n], rest[n:]
    me = lax.axis_index("gy")
    lane, sub = lane_index(), row_index()
    blocks = strip_rows // ROWS
    for h, owner in ((1, n - 1), (0, 0)):
        block = blocks - 1 if h else 0
        for k in range(n):

            @pl.when(lax.rem(me - k + n, n) == owner)
            def _():
                control = controls[k]
                for a in range(5):
                    for t in range(2):
                        if a == 0:
                            rim[h, a, t] = control[pl.ds(t * strip_rows + block * ROWS, ROWS), :]
                            continue
                        both = control[pl.ds(2 * strip_rows + ((a - 1) % 2 * 2 + t) * ROWS, ROWS), :]
                        rim[h, a, t] = both if a < 3 else pltpu.roll(both, 4, 0)
                    part, slot = rim_slot(a, block, blocks)
                    packed = control[pl.ds(2 * strip_rows + EDGE_ROWS + part * ROWS, ROWS), :]
                    rim[h, a, 2] = strip_columns(lane, packed, slot)

    for message, h in ((up, 1), (down, 0)):
        left, right = sides_at(n, strip_rows, controls, h * (HALF - ROWS))

        def field(a, t):
            if a >= TILE_FIELDS:
                return rim[h, a - TILE_FIELDS, t]
            if t == 2:
                return side_columns(lane, left, right, h * TILE_FIELDS + a)
            if a == TILE_FIELDS - 1:
                return jnp.full((ROWS, LANES), mask[h, t].astype(jnp.float32))
            return tile_field(a, state, visc, surf)[t, pl.ds(TILE if h else ROWS, ROWS), :]

        own = sub >= 4 if h else sub < 4
        for a in range(PAIRS):
            for t in range(3):
                message[a, t] = jnp.where(own, field(a, t), pltpu.roll(field(a + PAIRS, t), 4, 0))


def rim_rows(message, a, t):
    if a < PAIRS:
        return message[a, t]
    return pltpu.roll(message[a - PAIRS, t], 4, 0)


E_, N_, S_, U_, V_, K0_, K1_, I0_, I1_ = range(9)


def coefficients(coef, visc, ice, fric, lane):
    def step(i, carry):
        r = FIRST + i * ROWS
        rows, east, west = pl.ds(r, ROWS), pl.ds(r + 1, ROWS), pl.ds(r - 1, ROWS)
        cells = [ice[t, rows, :] for t in range(3)]
        layers = [[visc[l, t, rows, :] for t in range(3)] for l in range(LAYERS)]
        for l in range(LAYERS):
            centre = layers[l]
            north, south = after(centre, lane), before(centre, lane)
            for t in range(3):
                c = centre[t]
                e = 0.5 * (c + visc[l, t, east, :])
                w = 0.5 * (c + visc[l, t, west, :])
                nf = 0.5 * (c + north[t])
                sf = 0.5 * (c + south[t])
                coef[l, E_, t, rows, :] = e
                coef[l, N_, t, rows, :] = nf
                coef[l, S_, t, rows, :] = sf
                vertical = None
                if l < LAYERS - 1:
                    u = (0.5 * VERTICAL) * (c + layers[l + 1][t])
                    coef[l, U_, t, rows, :] = u
                    vertical = u
                if l > 0:
                    lower = (0.5 * VERTICAL) * (c + layers[l - 1][t])
                    vertical = lower if vertical is None else vertical + lower
                if l == 0:
                    vertical = vertical + fric[t, rows, :]
                coef[l, V_, t, rows, :] = (0.25 * COUPLING) * c
                rest = COUPLING * c + (1.0 - cells[t])
                ew, ns = e + w, nf + sf
                for c_, ax, ay in ((0, 4.0, 1.0), (1, 1.0, 4.0)):
                    own = (ax * ew if ax != 1.0 else ew) + (ay * ns if ay != 1.0 else ns) + vertical
                    inverse = DAMPING * cells[t] / (own + rest)
                    coef[l, I0_ + c_, t, rows, :] = inverse
                    coef[l, K0_ + c_, t, rows, :] = cells[t] - own * inverse
        return carry

    lax.fori_loop(0, STEPS, step, 0, unroll=STEPS)


def sweep_layer(coef, old, new, l, lane, force=None, last=False):
    first, steps, tiles = (ROWS, BLOCKS, 2) if last else (FIRST, STEPS, 3)

    def step(i, carry):
        r = first + i * ROWS
        rows, east, west = pl.ds(r, ROWS), pl.ds(r + 1, ROWS), pl.ds(r - 1, ROWS)
        e = [coef[l, E_, t, rows, :] for t in range(tiles)]
        w = [coef[l, E_, t, west, :] for t in range(tiles)]
        fluxes, mixes = [], []
        for c in range(2):
            m = [old(c, l)[t, rows, :] for t in range(3)]
            me = [old(c, l)[t, east, :] for t in range(3)]
            mw = [old(c, l)[t, west, :] for t in range(3)]
            mn, ms = after(m, lane), before(m, lane)
            across = [me[t] - mw[t] for t in range(3)]
            an, as_ = after(across, lane), before(across, lane)
            mixes.append([an[t] - as_[t] for t in range(tiles)])
            flux = []
            for t in range(tiles):
                x = e[t] * me[t] + w[t] * mw[t]
                y = coef[l, N_, t, rows, :] * mn[t] + coef[l, S_, t, rows, :] * ms[t]
                total = 4.0 * x + y if c == 0 else x + 4.0 * y
                if l < LAYERS - 1:
                    total = total + coef[l, U_, t, rows, :] * old(c, l + 1)[t, rows, :]
                if l > 0:
                    total = total + coef[l - 1, U_, t, rows, :] * old(c, l - 1)[t, rows, :]
                if force is not None:
                    total = total + force[c, t, rows, :]
                flux.append((total, m[t]))
            fluxes.append(flux)
        for c in range(2):
            for t in range(tiles):
                total, m = fluxes[c][t]
                total = total + coef[l, V_, t, rows, :] * mixes[1 - c][t]
                new(c, l)[t, rows, :] = (
                    coef[l, K0_ + c, t, rows, :] * m + coef[l, I0_ + c, t, rows, :] * total
                )
        return carry

    lax.fori_loop(0, steps, step, 0, unroll=steps)


def layers_of(ref):
    return lambda c, l: ref.at[c * LAYERS + l]


def before_forcing(n, strip_rows, mask, state_in, visc_in, surf_in, base, above, below, *rest):
    controls = rest[:n]
    s0, visc, surf, coef, s1, s2, s3, bottom, terms, reach, force = rest[n : n + 11]
    ice, logf, fric, bed, sems = rest[n + 11 :]
    me, mx = lax.axis_index("gy"), lax.axis_index("gx")
    size_x = lax.axis_size("gx")
    lane = lane_index()
    blocks = strip_rows // ROWS
    copies = start_copies(sems, [(base.at[:, :, pl.ds(t * LANES, LANES)], bed.at[:, t]) for t in range(2)])

    for h in range(2):
        for t in range(2):
            ice[t, pl.ds(ROWS + h * HALF, HALF), :] = jnp.full((HALF, LANES), mask[h, t].astype(jnp.float32))
    for message, row in ((above, 0), (below, ROWS + TILE)):
        rows = pl.ds(row, ROWS)
        for t in range(3):
            for a in range(8):
                s0[a, t, rows, :] = rim_rows(message, a, t)
            for a in range(4):
                visc[a, t, rows, :] = rim_rows(message, 8 + a, t)
            ice[t, rows, :] = rim_rows(message, 14, t)
            logf[t, rows, :] = rim_rows(message, 15, t)
            for c in range(2):
                difference = rim_rows(message, 16 + c, t) - rim_rows(message, 12 + c, t)
                force[c, t, rows, :] = rim_rows(message, 18 + c, t) * difference

    def sides(r, carry):
        left, right = sides_at(n, strip_rows, controls, r * ROWS)
        for h in range(2):
            to = pl.ds(pl.multiple_of(ROWS + h * HALF + r * ROWS, ROWS), ROWS)
            for a in range(TILE_FIELDS):
                value = side_columns(lane, left, right, h * TILE_FIELDS + a)
                if a == TILE_FIELDS - 1:
                    ice[2, to, :] = value
                else:
                    tile_field(a, s0, visc, surf)[2, to, :] = value
        return carry

    lax.fori_loop(0, HALF // ROWS, sides, 0, unroll=8)
    for k in range(n):
        source = lax.rem(me - k + n, n)
        for b in range(blocks):
            to = pl.ds(pl.multiple_of(ROWS + source * strip_rows + b * ROWS, ROWS), ROWS)
            for t in range(2):
                logf[t, to, :] = controls[k][pl.ds(t * strip_rows + b * ROWS, ROWS), :]
            values = []
            for a in range(5):
                part, slot = rim_slot(a, b, blocks)
                packed = controls[k][pl.ds(2 * strip_rows + EDGE_ROWS + part * ROWS, ROWS), :]
                values.append(strip_columns(lane, packed, slot))
            logf[2, to, :] = values[0]
            for c in range(2):
                force[c, 2, to, :] = values[3 + c] * (values[1 + c] - surf[c, 2, to, :])
    for i in range(FRAME // ROWS):
        rows = pl.ds(i * ROWS, ROWS)
        for t in range(3):
            fric[t, rows, :] = jnp.exp(logf[t, rows, :])
    coefficients(coef, visc, ice, fric, lane)
    steps = [layers_of(s) for s in (s0, s1, s2, s3)] + [lambda c, l: bottom.at[c]]
    for sweep in range(SWEEPS):
        for l in range(LAYERS - sweep):
            sweep_layer(coef, steps[sweep], steps[sweep + 1], l, lane, last=sweep == SWEEPS - 1)
    for copy in copies:
        copy.wait()

    def finish(i, carry):
        r = pl.multiple_of(i * ROWS, ROWS)
        rows, east, west = pl.ds(r + ROWS, ROWS), pl.ds(r + ROWS + 1, ROWS), pl.ds(r + ROWS - 1, ROWS)
        centre = [logf[t, rows, :] for t in range(3)]
        north, south = after(centre, lane), before(centre, lane)
        row = row_index() + r
        in_west = jnp.logical_or(row != 0, mx != 0)
        in_east = jnp.logical_or(row != TILE - 1, mx != size_x - 1)
        in_south = jnp.logical_or(lane != 0, me != 0)
        in_north = jnp.logical_or(lane != LANES - 1, me != n - 1)
        inner = pl.ds(r, ROWS)
        for t in range(2):
            c = centre[t]
            smooth = jnp.where(in_west, c - logf[t, west, :], 0.0) + jnp.where(in_east, c - logf[t, east, :], 0.0)
            left, right = c - south[t], c - north[t]
            smooth = smooth + (jnp.where(in_south, left, 0.0) if t == 0 else left)
            smooth = smooth + (jnp.where(in_north, right, 0.0) if t == 1 else right)
            total = TIKHONOV * smooth
            for component in range(2):
                along = coef[LAYERS - 1, I0_ + component, t, rows, :]
                for l in (2, 1, 0):
                    along = along * (coef[l, I0_ + component, t, rows, :] * coef[l, U_, t, rows, :])
                reach[component, t, inner, :] = along
                weight = fric[t, rows, :] * bed[component, t, inner, :]
                total = total + weight * bottom[component, t, rows, :]
                terms[1 + component, t, inner, :] = weight * along
            terms[0, t, inner, :] = total
        return carry

    lax.fori_loop(0, BLOCKS, finish, 0, unroll=8)


def gradient_kernel(n, strip_rows, terms, surf, rims, *rest):
    datas, force, grads = rest[:n], rest[n], rest[n + 1 :]
    me = lax.axis_index("gy")
    for k in range(n):
        source = lax.rem(me - k + n, n)
        for b in range(strip_rows // ROWS):
            row = source * strip_rows + b * ROWS
            inner = pl.ds(pl.multiple_of(row, ROWS), ROWS)
            rows = pl.ds(pl.multiple_of(ROWS + row, ROWS), ROWS)
            part = pl.ds(b * ROWS, ROWS)
            for t in range(2):
                total = terms[0, t, inner, :]
                for c in range(2):
                    value = datas[k][2 + c, t, part, :] * (datas[k][c, t, part, :] - surf[c, t, rows, :])
                    force[c, t, rows, :] = value
                    total = total + terms[1 + c, t, inner, :] * value
                grads[k][t, part, :] = total


def after_forcing(coef, s1, s2, s3, bottom, reach, force, out, n1, n2, n3, n4, sems):
    lane = lane_index()
    copies = []

    def send(l):
        for c in range(2):
            for t in range(2):
                source = n4.at[c * LAYERS + l, t, pl.ds(ROWS, TILE), :]
                target = out.at[c * LAYERS + l, :, pl.ds(t * LANES, LANES)]
                copy = pltpu.make_async_copy(source, target, sems.at[len(copies)])
                copy.start()
                copies.append(copy)

    for i in range(BLOCKS):
        rows, inner = pl.ds(ROWS + i * ROWS, ROWS), pl.ds(i * ROWS, ROWS)
        for t in range(2):
            for c in range(2):
                n4[c * LAYERS, t, rows, :] = bottom[c, t, rows, :] + reach[c, t, inner, :] * force[c, t, rows, :]
    send(0)

    def add_forcing(i, carry):
        rows = pl.ds(FIRST + i * ROWS, ROWS)
        for t in range(3):
            for c in range(2):
                value = coef[3, I0_ + c, t, rows, :] * force[c, t, rows, :]
                n1[c, t, rows, :] = s1[c * LAYERS + 3, t, rows, :] + value
                value = coef[2, I0_ + c, t, rows, :] * (coef[2, U_, t, rows, :] * value)
                n2[2 * c, t, rows, :] = s2[c * LAYERS + 2, t, rows, :] + value
                value = coef[1, I0_ + c, t, rows, :] * (coef[1, U_, t, rows, :] * value)
                n3[3 * c, t, rows, :] = s3[c * LAYERS + 1, t, rows, :] + value
        return carry

    lax.fori_loop(0, STEPS, add_forcing, 0, unroll=STEPS)

    def first(c, l):
        return n1.at[c] if l == 3 else s1.at[c * LAYERS + l]

    def second(c, l):
        return n2.at[2 * c + l - 2] if l >= 2 else s2.at[c * LAYERS + l]

    def third(c, l):
        return n3.at[3 * c + l - 1] if l >= 1 else s3.at[c * LAYERS + l]

    sweep_layer(coef, first, second, 3, lane, force)
    sweep_layer(coef, second, third, 2, lane)
    sweep_layer(coef, second, third, 3, lane, force)
    for l in (1, 2, 3):
        sweep_layer(coef, third, layers_of(n4), l, lane, force if l == 3 else None, last=True)
        send(l)
    for copy in copies:
        copy.wait()


def unpack_gradient(n, *refs):
    parts, out = refs[:n], refs[n]
    me = lax.axis_index("gy")
    for k in range(n):
        source = lax.rem(me + k, n)
        for t in range(2):
            out[:, pl.ds(pl.multiple_of(source * TILE + t * LANES, LANES), LANES)] = parts[k][t]


def f32(*shape):
    return jax.ShapeDtypeStruct(shape, jnp.float32)


def vmem_f32(*shape):
    return pltpu.VMEM(shape, jnp.float32)


def frames(*leading):
    return vmem_f32(*leading, 3, FRAME, LANES)


def in_vmem(x):
    return pltpu.with_memory_space_constraint(x, pltpu.VMEM)


def in_hbm(x):
    return pltpu.with_memory_space_constraint(x, pltpu.HBM)


def per_device(
    adjoint_start,
    viscosity,
    base_velocity,
    surface_velocity,
    ice_mask,
    log_friction,
    observed_velocity,
    obs_weight,
):
    n = lax.axis_size("gy")
    size_x = lax.axis_size("gx")
    strip_rows = log_friction.shape[0]
    width = n * TILE
    vmem = pl.BlockSpec(memory_space=pltpu.VMEM)
    smem = pl.BlockSpec(memory_space=pltpu.SMEM)
    anywhere = pl.BlockSpec(memory_space=pl.ANY)
    ice_mask = in_hbm(ice_mask)
    adjoint = adjoint_start.reshape((2 * LAYERS, TILE, TILE))

    def params(mib):
        return pltpu.CompilerParams(vmem_limit_bytes=mib * MIB)

    def ring(k):
        return [(i, (i + k) % n) for i in range(n)]

    def line(size, k):
        return [(i, i + k) for i in range(size) if 0 <= i + k < size]

    def control_shape(k):
        return f32(control_rows(strip_rows) + (HALF if k in (1, n - 1) else 0), LANES)

    *controls, state, visc, surf = pl.pallas_call(
        functools.partial(pack_kernel, n, strip_rows),
        out_shape=[control_shape(k) for k in range(n)] + [frames(2 * LAYERS), frames(LAYERS), frames(2)],
        in_specs=[smem] + [anywhere] * 6,
        out_specs=[vmem] * (n + 3),
        scratch_shapes=[
            vmem_f32(strip_rows, width),
            vmem_f32(2, strip_rows, width),
            vmem_f32(2, strip_rows, width),
            pltpu.SemaphoreType.DMA((3 + 12 * CHUNKS,)),
        ],
        compiler_params=params(6),
    )(
        ice_mask,
        in_hbm(log_friction),
        in_hbm(observed_velocity),
        in_hbm(obs_weight),
        in_hbm(adjoint),
        in_hbm(viscosity),
        in_hbm(surface_velocity),
    )
    state, visc, surf = in_vmem(state), in_vmem(visc), in_vmem(surf)
    controls, observed_velocity, obs_weight = lax.optimization_barrier((controls, observed_velocity, obs_weight))
    datas = pl.pallas_call(
        functools.partial(pack_observations, n, strip_rows),
        out_shape=[f32(4, 2, strip_rows, LANES)] * n,
        in_specs=[anywhere] * 2,
        out_specs=[anywhere] * n,
        scratch_shapes=[vmem_f32(2, strip_rows, width)] * 2 + [pltpu.SemaphoreType.DMA((4 * n,))],
        compiler_params=params(8),
    )(in_hbm(observed_velocity), in_hbm(obs_weight))
    datas = list(datas)
    controls = [controls[0]] + [lax.ppermute(controls[k], "gy", ring(k)) for k in range(1, n)]
    controls, sent = lax.optimization_barrier((controls, datas[1:]))
    datas = [datas[0]] + [lax.ppermute(sent[k - 1], "gy", ring(k)) for k in range(1, n)]

    rows_up, rows_down = pl.pallas_call(
        functools.partial(pack_rows, n, strip_rows),
        out_shape=[f32(PAIRS, 3, ROWS, LANES)] * 2,
        in_specs=[smem] + [vmem] * (3 + n),
        out_specs=[vmem] * 2,
        scratch_shapes=[vmem_f32(2, 5, 3, ROWS, LANES)],
        compiler_params=params(4),
    )(ice_mask, state, visc, surf, *controls)
    above = lax.ppermute(rows_up, "gx", line(size_x, 1))
    below = lax.ppermute(rows_down, "gx", line(size_x, -1))

    _, _, surf, *held, force = pl.pallas_call(
        functools.partial(before_forcing, n, strip_rows),
        out_shape=[
            frames(2 * LAYERS),
            frames(LAYERS),
            frames(2),
            frames(LAYERS, 9),
            frames(2 * LAYERS),
            frames(2 * LAYERS),
            frames(2 * LAYERS),
            vmem_f32(2, 2, FRAME, LANES),
            vmem_f32(3, 2, TILE, LANES),
            vmem_f32(2, 2, TILE, LANES),
            frames(2),
        ],
        in_specs=[smem] + [vmem] * 3 + [anywhere] + [vmem] * (2 + n),
        out_specs=[vmem] * 11,
        scratch_shapes=[
            frames(),
            frames(),
            frames(),
            vmem_f32(2, 2, TILE, LANES),
            pltpu.SemaphoreType.DMA((2,)),
        ],
        input_output_aliases={1: 0, 2: 1, 3: 2},
        compiler_params=params(12),
    )(ice_mask, state, visc, surf, in_hbm(base_velocity), above, below, *controls)
    coef, s1, s2, s3, bottom, terms, reach = [in_vmem(x) for x in held]

    force, *grads = pl.pallas_call(
        functools.partial(gradient_kernel, n, strip_rows),
        out_shape=[frames(2)] + [f32(2, strip_rows, LANES)] * n,
        in_specs=[vmem] * (3 + n),
        out_specs=[vmem] * (1 + n),
        input_output_aliases={2: 0},
        compiler_params=params(6),
    )(terms, in_vmem(surf), in_vmem(force), *datas)
    parts = [grads[0]] + [lax.ppermute(grads[k], "gy", ring(n - k)) for k in range(1, n)]

    out = pl.pallas_call(
        after_forcing,
        out_shape=f32(2 * LAYERS, TILE, TILE),
        in_specs=[vmem] * 7,
        out_specs=anywhere,
        scratch_shapes=[
            frames(2),
            frames(4),
            frames(6),
            vmem_f32(2 * LAYERS, 2, FRAME, LANES),
            pltpu.SemaphoreType.DMA((16,)),
        ],
        compiler_params=params(12),
    )(coef, s1, s2, s3, bottom, reach, in_vmem(force))

    gradient = pl.pallas_call(
        functools.partial(unpack_gradient, n),
        out_shape=f32(strip_rows, width),
        in_specs=[vmem] * n,
        out_specs=vmem,
        compiler_params=params(4),
    )(*parts)
    return gradient, out.reshape(adjoint_start.shape)


def solution(mesh):
    placed = (
        P(None, None, "gx", "gy"),
        P(None, "gx", "gy"),
        P(None, "gx", "gy"),
        P(None, "gx", "gy"),
        P("gx", "gy"),
        P(("gx", "gy"), None),
        P(None, ("gx", "gy"), None),
        P(None, ("gx", "gy"), None),
    )
    return jax.shard_map(
        per_device,
        mesh=mesh,
        in_specs=placed,
        out_specs=(P(("gx", "gy"), None), P(None, None, "gx", "gy")),
        check_vma=False,
    )
```

```python
import functools

import jax
import jax.numpy as jnp
from jax import lax
from jax.experimental import pallas as pl
from jax.experimental.pallas import tpu as pltpu
from jax.sharding import PartitionSpec as P

SWEEPS = 4
DAMPING = 0.8
VERTICAL = 2.0
COUPLING = 3.0
TIKHONOV = 0.25

LAYERS = 4
LANES = 128
ROWS = 8
TILE = 256
FRAME = TILE + 2 * ROWS
HALF = TILE // 2
BLOCKS = TILE // ROWS
FIRST = 4
STEPS = BLOCKS + 1
TILE_FIELDS = 15
RIM_FIELDS = 20
PAIRS = RIM_FIELDS // 2
EDGE_ROWS = 4 * ROWS
MIB = 1024 * 1024


def row_index():
    return lax.broadcasted_iota(jnp.int32, (ROWS, LANES), 0)


def lane_index():
    return lax.broadcasted_iota(jnp.int32, (ROWS, LANES), 1)


def roll_to(x, shift):
    shift = shift % LANES
    return x if shift == 0 else pltpu.roll(x, shift, 1)


def after(x, lane):
    a, b, c = (roll_to(v, -1) for v in x)
    last = lane == LANES - 1
    return jnp.where(last, b, a), jnp.where(last, c, b), jnp.where(last, a, c)


def before(x, lane):
    a, b, c = (roll_to(v, 1) for v in x)
    first = lane == 0
    return jnp.where(first, c, a), jnp.where(first, a, b), jnp.where(first, b, c)


def rim_slot(array, block, strip_blocks):
    position = array * strip_blocks + block
    return position // 16, position % 16


def rim_tiles(strip_rows):
    return -(-5 * (strip_rows // ROWS) // 16)


def control_rows(strip_rows):
    return 2 * strip_rows + EDGE_ROWS + ROWS * rim_tiles(strip_rows)


def pack_strips(n, strip_rows, logf, obs, weight, controls):
    me = lax.axis_index("gy")
    lane = lane_index()
    blocks = strip_rows // ROWS
    edge = pl.multiple_of(jnp.where(me == 0, 0, strip_rows - ROWS), ROWS)
    own = (row_index() < 4) == (me == 0)
    strips = [logf.at[...], obs.at[0], obs.at[1], weight.at[0], weight.at[1]]
    width = n * TILE
    for k in range(n):
        to = lax.rem(me + k, n)
        column = pl.multiple_of(to * TILE, TILE)
        left = pl.multiple_of(jnp.maximum(column - LANES, 0), LANES)
        right = pl.multiple_of(jnp.minimum(column + TILE, width - LANES), LANES)
        control = controls[k]
        for t in range(2):
            columns = pl.ds(column + t * LANES, LANES)
            control[pl.ds(t * strip_rows, strip_rows), :] = logf[:, columns]
            for a in range(2):
                ends = [strips[a + i][pl.ds(edge, ROWS), columns] for i in (1, 3)]
                both = jnp.where(own, ends[0], pltpu.roll(ends[1], 4, 0))
                control[pl.ds(2 * strip_rows + (a * 2 + t) * ROWS, ROWS), :] = both
        packed = [jnp.zeros((ROWS, LANES), jnp.float32) for _ in range(rim_tiles(strip_rows))]
        for a in range(5):
            for b in range(blocks):
                part, slot = rim_slot(a, b, blocks)
                rows = pl.ds(b * ROWS, ROWS)
                both = jnp.where(lane < 64, strips[a][rows, pl.ds(right, LANES)], strips[a][rows, pl.ds(left, LANES)])
                packed[part] = jnp.where(lane // 8 == slot, roll_to(both, 8 * slot + 4), packed[part])
        for part, value in enumerate(packed):
            control[pl.ds(2 * strip_rows + EDGE_ROWS + part * ROWS, ROWS), :] = value


def tile_field(a, state, visc, surf):
    if a < 8:
        return state.at[a]
    if a < 12:
        return visc.at[a - 8]
    return surf.at[a - 12]


CHUNKS = 2


def pack_columns(mask, state, visc, surf, up, down, first, chunk):
    lane = lane_index()
    count = HALF // ROWS // CHUNKS
    for r in range(chunk * count, (chunk + 1) * count):
        to_up = jnp.zeros((ROWS, LANES), jnp.float32)
        to_down = jnp.zeros((ROWS, LANES), jnp.float32)
        for h in range(2):
            rows = pl.ds(ROWS + h * HALF + r * ROWS, ROWS)
            for a in range(TILE_FIELDS):
                slot = h * TILE_FIELDS + a
                here = lane // 4 == slot
                if a == TILE_FIELDS - 1:
                    low = mask[h, 0].astype(jnp.float32)
                    high = mask[h, 1].astype(jnp.float32)
                    to_up = jnp.where(here, high, to_up)
                    to_down = jnp.where(here, low, to_down)
                else:
                    field = tile_field(a, state, visc, surf)
                    to_up = jnp.where(here, roll_to(field[1, rows, :], 4 * slot + 4), to_up)
                    to_down = jnp.where(here, roll_to(field[0, rows, :], 4 * slot), to_down)
        rows = pl.ds(first + r * ROWS, ROWS)
        up[rows, :] = to_up
        down[rows, :] = to_down


def start_copies(sems, pairs):
    copies = [pltpu.make_async_copy(source, target, sems.at[i]) for i, (source, target) in enumerate(pairs)]
    for copy in copies:
        copy.start()
    return copies


def pack_kernel(n, strip_rows, mask, logf, obs, weight, adjoint, viscosity, surface, *rest):
    controls, (state, visc, surf, logf_in, obs_in, weight_in, sems) = rest[:n], rest[n:]
    pairs = [(logf, logf_in), (obs, obs_in), (weight, weight_in)]
    size = HALF // CHUNKS
    for chunk in range(CHUNKS):
        for h in range(2):
            row = h * HALF + chunk * size
            for field, frame in ((adjoint, state), (viscosity, visc), (surface, surf)):
                for t in range(2):
                    source = field.at[:, pl.ds(row, size), pl.ds(t * LANES, LANES)]
                    pairs.append((source, frame.at[:, t, pl.ds(ROWS + row, size), :]))
    copies = start_copies(sems, pairs)
    for copy in copies[:3]:
        copy.wait()
    pack_strips(n, strip_rows, logf_in, obs_in, weight_in, controls)
    first = control_rows(strip_rows)
    for chunk in range(CHUNKS):
        for copy in copies[3 + 12 * chunk : 15 + 12 * chunk]:
            copy.wait()
        pack_columns(mask, state, visc, surf, controls[1], controls[n - 1], first, chunk)


def pack_observations(n, strip_rows, obs, weight, *rest):
    datas, (obs_in, weight_in, sems) = rest[:n], rest[n:]
    me = lax.axis_index("gy")
    for copy in start_copies(sems, [(obs, obs_in), (weight, weight_in)]):
        copy.wait()
    pairs = []
    for k in range(n):
        column = pl.multiple_of(lax.rem(me + k, n) * TILE, TILE)
        for t in range(2):
            columns = pl.ds(column + t * LANES, LANES)
            pairs.append((obs_in.at[:, :, columns], datas[k].at[0:2, t]))
            pairs.append((weight_in.at[:, :, columns], datas[k].at[2:4, t]))
    for copy in start_copies(sems, pairs):
        copy.wait()


def side_columns(lane, from_left, from_right, slot):
    left = roll_to(from_left, -(4 * slot + 4))
    right = roll_to(from_right, -4 * slot)
    return jnp.where(lane < 4, right, jnp.where(lane >= LANES - 4, left, 0.0))


def strip_columns(lane, packed, slot):
    value = roll_to(packed, -(8 * slot + 4))
    return jnp.where(jnp.logical_or(lane < 4, lane >= LANES - 4), value, 0.0)


def sides_at(n, strip_rows, controls, row):
    me = lax.axis_index("gy")
    rows = pl.ds(pl.multiple_of(control_rows(strip_rows) + row, ROWS), ROWS)
    left = jnp.where(me > 0, controls[1][rows, :], 0.0)
    right = jnp.where(me < n - 1, controls[n - 1][rows, :], 0.0)
    return left, right


def pack_rows(n, strip_rows, mask, state, visc, surf, *rest):
    controls, (up, down, rim) = rest[:n], rest[n:]
    me = lax.axis_index("gy")
    lane, sub = lane_index(), row_index()
    blocks = strip_rows // ROWS
    for h, owner in ((1, n - 1), (0, 0)):
        block = blocks - 1 if h else 0
        for k in range(n):

            @pl.when(lax.rem(me - k + n, n) == owner)
            def _():
                control = controls[k]
                for a in range(5):
                    for t in range(2):
                        if a == 0:
                            rim[h, a, t] = control[pl.ds(t * strip_rows + block * ROWS, ROWS), :]
                            continue
                        both = control[pl.ds(2 * strip_rows + ((a - 1) % 2 * 2 + t) * ROWS, ROWS), :]
                        rim[h, a, t] = both if a < 3 else pltpu.roll(both, 4, 0)
                    part, slot = rim_slot(a, block, blocks)
                    packed = control[pl.ds(2 * strip_rows + EDGE_ROWS + part * ROWS, ROWS), :]
                    rim[h, a, 2] = strip_columns(lane, packed, slot)

    for message, h in ((up, 1), (down, 0)):
        left, right = sides_at(n, strip_rows, controls, h * (HALF - ROWS))

        def field(a, t):
            if a >= TILE_FIELDS:
                return rim[h, a - TILE_FIELDS, t]
            if t == 2:
                return side_columns(lane, left, right, h * TILE_FIELDS + a)
            if a == TILE_FIELDS - 1:
                return jnp.full((ROWS, LANES), mask[h, t].astype(jnp.float32))
            return tile_field(a, state, visc, surf)[t, pl.ds(TILE if h else ROWS, ROWS), :]

        own = sub >= 4 if h else sub < 4
        for a in range(PAIRS):
            for t in range(3):
                message[a, t] = jnp.where(own, field(a, t), pltpu.roll(field(a + PAIRS, t), 4, 0))


def rim_rows(message, a, t):
    if a < PAIRS:
        return message[a, t]
    return pltpu.roll(message[a - PAIRS, t], 4, 0)


E_, N_, S_, U_, V_, K0_, K1_, I0_, I1_ = range(9)


def over_blocks(step, count, ends):
    if ends:
        for i in (0, count - 1):
            step(i, 0)
    else:
        lax.fori_loop(0, count, step, 0, unroll=True)


def coefficients(coef, visc, ice, fric, lane, ends):
    def step(i, carry):
        r = FIRST + i * ROWS
        rows, east, west = pl.ds(r, ROWS), pl.ds(r + 1, ROWS), pl.ds(r - 1, ROWS)
        cells = [ice[t, rows, :] for t in range(3)]
        layers = [[visc[l, t, rows, :] for t in range(3)] for l in range(LAYERS)]
        for l in range(LAYERS):
            centre = layers[l]
            north, south = after(centre, lane), before(centre, lane)
            for t in range(3):
                c = centre[t]
                e = 0.5 * (c + visc[l, t, east, :])
                w = 0.5 * (c + visc[l, t, west, :])
                nf = 0.5 * (c + north[t])
                sf = 0.5 * (c + south[t])
                coef[l, E_, t, rows, :] = e
                coef[l, N_, t, rows, :] = nf
                coef[l, S_, t, rows, :] = sf
                vertical = None
                if l < LAYERS - 1:
                    u = (0.5 * VERTICAL) * (c + layers[l + 1][t])
                    coef[l, U_, t, rows, :] = u
                    vertical = u
                if l > 0:
                    lower = (0.5 * VERTICAL) * (c + layers[l - 1][t])
                    vertical = lower if vertical is None else vertical + lower
                if l == 0:
                    vertical = vertical + fric[t, rows, :]
                coef[l, V_, t, rows, :] = (0.25 * COUPLING) * c
                rest = COUPLING * c + (1.0 - cells[t])
                ew, ns = e + w, nf + sf
                for c_, ax, ay in ((0, 4.0, 1.0), (1, 1.0, 4.0)):
                    own = (ax * ew if ax != 1.0 else ew) + (ay * ns if ay != 1.0 else ns) + vertical
                    inverse = DAMPING * cells[t] / (own + rest)
                    coef[l, I0_ + c_, t, rows, :] = inverse
                    coef[l, K0_ + c_, t, rows, :] = cells[t] - own * inverse
        return carry

    over_blocks(step, STEPS, ends)


def sweep_layer(coef, old, new, l, lane, force=None, last=False, ends=False):
    first, steps, tiles = (ROWS, BLOCKS, 2) if last else (FIRST, STEPS, 3)

    def step(i, carry):
        r = first + i * ROWS
        rows, east, west = pl.ds(r, ROWS), pl.ds(r + 1, ROWS), pl.ds(r - 1, ROWS)
        e = [coef[l, E_, t, rows, :] for t in range(tiles)]
        w = [coef[l, E_, t, west, :] for t in range(tiles)]
        fluxes, mixes = [], []
        for c in range(2):
            m = [old(c, l)[t, rows, :] for t in range(3)]
            me = [old(c, l)[t, east, :] for t in range(3)]
            mw = [old(c, l)[t, west, :] for t in range(3)]
            mn, ms = after(m, lane), before(m, lane)
            across = [me[t] - mw[t] for t in range(3)]
            an, as_ = after(across, lane), before(across, lane)
            mixes.append([an[t] - as_[t] for t in range(tiles)])
            flux = []
            for t in range(tiles):
                x = e[t] * me[t] + w[t] * mw[t]
                y = coef[l, N_, t, rows, :] * mn[t] + coef[l, S_, t, rows, :] * ms[t]
                total = 4.0 * x + y if c == 0 else x + 4.0 * y
                if l < LAYERS - 1:
                    total = total + coef[l, U_, t, rows, :] * old(c, l + 1)[t, rows, :]
                if l > 0:
                    total = total + coef[l - 1, U_, t, rows, :] * old(c, l - 1)[t, rows, :]
                if force is not None:
                    total = total + force[c, t, rows, :]
                flux.append((total, m[t]))
            fluxes.append(flux)
        for c in range(2):
            for t in range(tiles):
                total, m = fluxes[c][t]
                total = total + coef[l, V_, t, rows, :] * mixes[1 - c][t]
                new(c, l)[t, rows, :] = (
                    coef[l, K0_ + c, t, rows, :] * m + coef[l, I0_ + c, t, rows, :] * total
                )
        return carry

    over_blocks(step, steps, ends)


GROUP = 4


def sweep_reached(coef, work, old, new, l, lane, force=None, last=False):
    first, steps, tiles = (ROWS, BLOCKS, 2) if last else (FIRST, STEPS, 3)

    def along_y(i, carry):
        rows = pl.ds(i * ROWS, ROWS)
        for c in range(2):
            m = [old(c, l)[t, rows, :] for t in range(3)]
            mn, ms = after(m, lane), before(m, lane)
            for t in range(tiles):
                y = coef[l, N_, t, rows, :] * mn[t] + coef[l, S_, t, rows, :] * ms[t]
                work[0, c, t, rows, :] = 4.0 * y if c else y
                work[1, c, t, rows, :] = mn[t] - ms[t]
        return carry

    lax.fori_loop(0, FRAME // ROWS, along_y, 0, unroll=True)

    def block(i):
        r = first + i * ROWS
        rows, east, west = pl.ds(r, ROWS), pl.ds(r + 1, ROWS), pl.ds(r - 1, ROWS)
        for t in range(tiles):
            e, w = coef[l, E_, t, rows, :], coef[l, E_, t, west, :]
            for c in range(2):
                x = e * old(c, l)[t, east, :] + w * old(c, l)[t, west, :]
                total = (x if c else 4.0 * x) + work[0, c, t, rows, :]
                if l < LAYERS - 1:
                    total = total + coef[l, U_, t, rows, :] * old(c, l + 1)[t, rows, :]
                if l > 0:
                    total = total + coef[l - 1, U_, t, rows, :] * old(c, l - 1)[t, rows, :]
                if force is not None:
                    total = total + force[c, t, rows, :]
                mixed = work[1, 1 - c, t, east, :] - work[1, 1 - c, t, west, :]
                total = total + coef[l, V_, t, rows, :] * mixed
                value = coef[l, K0_ + c, t, rows, :] * old(c, l)[t, rows, :] + coef[l, I0_ + c, t, rows, :] * total
                yield c, t, rows, value

    for start in range(0, steps, GROUP):
        results = [result for i in range(start, min(start + GROUP, steps)) for result in block(i)]
        for c, t, rows, value in results:
            new(c, l)[t, rows, :] = value


def layers_of(ref):
    return lambda c, l: ref.at[c * LAYERS + l]


def gradient_terms(n, coef, logf, fric, bed, bottom, terms, reach, lane, ends):
    me, mx = lax.axis_index("gy"), lax.axis_index("gx")
    size_x = lax.axis_size("gx")

    def finish(i, carry):
        r = i * ROWS
        rows, east, west = pl.ds(r + ROWS, ROWS), pl.ds(r + ROWS + 1, ROWS), pl.ds(r + ROWS - 1, ROWS)
        centre = [logf[t, rows, :] for t in range(3)]
        north, south = after(centre, lane), before(centre, lane)
        row = row_index() + r
        in_west = jnp.logical_or(row != 0, mx != 0)
        in_east = jnp.logical_or(row != TILE - 1, mx != size_x - 1)
        in_south = jnp.logical_or(lane != 0, me != 0)
        in_north = jnp.logical_or(lane != LANES - 1, me != n - 1)
        inner = pl.ds(r, ROWS)
        for t in range(2):
            c = centre[t]
            smooth = jnp.where(in_west, c - logf[t, west, :], 0.0) + jnp.where(in_east, c - logf[t, east, :], 0.0)
            left, right = c - south[t], c - north[t]
            smooth = smooth + (jnp.where(in_south, left, 0.0) if t == 0 else left)
            smooth = smooth + (jnp.where(in_north, right, 0.0) if t == 1 else right)
            total = TIKHONOV * smooth
            for component in range(2):
                along = coef[LAYERS - 1, I0_ + component, t, rows, :]
                for l in (2, 1, 0):
                    along = along * (coef[l, I0_ + component, t, rows, :] * coef[l, U_, t, rows, :])
                reach[component, t, inner, :] = along
                weight = fric[t, rows, :] * bed[component, t, inner, :]
                total = total + weight * bottom[component, t, rows, :]
                terms[1 + component, t, inner, :] = weight * along
            terms[0, t, inner, :] = total
        return carry

    over_blocks(finish, BLOCKS, ends)


def sweeps_without_forcing(coef, s0, s1, s2, s3, bottom, lane, ends):
    steps = [layers_of(s) for s in (s0, s1, s2, s3)] + [lambda c, l: bottom.at[c]]
    for sweep in range(SWEEPS):
        for l in range(LAYERS - sweep):
            sweep_layer(coef, steps[sweep], steps[sweep + 1], l, lane, last=sweep == SWEEPS - 1, ends=ends)


def before_forcing(n, strip_rows, mask, state_in, visc_in, surf_in, base, *rest):
    controls = rest[:n]
    s0, visc, surf, coef, s1, s2, s3, bottom, terms, reach, force, ice, logf, fric, bed, sems = rest[n:]
    me = lax.axis_index("gy")
    lane = lane_index()
    blocks = strip_rows // ROWS
    copies = start_copies(sems, [(base.at[:, :, pl.ds(t * LANES, LANES)], bed.at[:, t]) for t in range(2)])

    for h in range(2):
        for t in range(2):
            ice[t, pl.ds(ROWS + h * HALF, HALF), :] = jnp.full((HALF, LANES), mask[h, t].astype(jnp.float32))
    zero = jnp.zeros((ROWS, LANES), jnp.float32)
    for row in (0, ROWS + TILE):
        rows = pl.ds(row, ROWS)
        for t in range(3):
            for a in range(12):
                tile_field(a, s0, visc, surf)[t, rows, :] = zero
            ice[t, rows, :] = zero
            logf[t, rows, :] = zero

    def sides(r, carry):
        left, right = sides_at(n, strip_rows, controls, r * ROWS)
        for h in range(2):
            to = pl.ds(pl.multiple_of(ROWS + h * HALF + r * ROWS, ROWS), ROWS)
            for a in range(TILE_FIELDS):
                value = side_columns(lane, left, right, h * TILE_FIELDS + a)
                if a == TILE_FIELDS - 1:
                    ice[2, to, :] = value
                else:
                    tile_field(a, s0, visc, surf)[2, to, :] = value
        return carry

    lax.fori_loop(0, HALF // ROWS, sides, 0, unroll=8)
    for k in range(n):
        source = lax.rem(me - k + n, n)
        for b in range(blocks):
            to = pl.ds(pl.multiple_of(ROWS + source * strip_rows + b * ROWS, ROWS), ROWS)
            for t in range(2):
                logf[t, to, :] = controls[k][pl.ds(t * strip_rows + b * ROWS, ROWS), :]
            values = []
            for a in range(5):
                part, slot = rim_slot(a, b, blocks)
                packed = controls[k][pl.ds(2 * strip_rows + EDGE_ROWS + part * ROWS, ROWS), :]
                values.append(strip_columns(lane, packed, slot))
            logf[2, to, :] = values[0]
            for c in range(2):
                force[c, 2, to, :] = values[3 + c] * (values[1 + c] - surf[c, 2, to, :])
    for i in range(FRAME // ROWS):
        rows = pl.ds(i * ROWS, ROWS)
        for t in range(3):
            fric[t, rows, :] = jnp.exp(logf[t, rows, :])
    coefficients(coef, visc, ice, fric, lane, False)
    sweeps_without_forcing(coef, s0, s1, s2, s3, bottom, lane, False)
    for copy in copies:
        copy.wait()
    gradient_terms(n, coef, logf, fric, bed, bottom, terms, reach, lane, False)


def at_edges(n, bed, above, below, *rest):
    s0, visc, coef, s1, s2, s3, bottom, terms, reach, force, ice, logf, fric = rest[13:]
    lane = lane_index()
    for message, row in ((above, 0), (below, ROWS + TILE)):
        rows = pl.ds(row, ROWS)
        for t in range(3):
            for a in range(12):
                tile_field(a, s0, visc, None)[t, rows, :] = rim_rows(message, a, t)
            ice[t, rows, :] = rim_rows(message, 14, t)
            value = rim_rows(message, 15, t)
            logf[t, rows, :] = value
            fric[t, rows, :] = jnp.exp(value)
            for c in range(2):
                difference = rim_rows(message, 16 + c, t) - rim_rows(message, 12 + c, t)
                force[c, t, rows, :] = rim_rows(message, 18 + c, t) * difference
    coefficients(coef, visc, ice, fric, lane, True)
    sweeps_without_forcing(coef, s0, s1, s2, s3, bottom, lane, True)
    gradient_terms(n, coef, logf, fric, bed, bottom, terms, reach, lane, True)


def gradient_kernel(n, strip_rows, terms, surf, rims, *rest):
    datas, force, grads = rest[:n], rest[n], rest[n + 1 :]
    me = lax.axis_index("gy")
    for k in range(n):
        source = lax.rem(me - k + n, n)
        for b in range(strip_rows // ROWS):
            row = source * strip_rows + b * ROWS
            inner = pl.ds(pl.multiple_of(row, ROWS), ROWS)
            rows = pl.ds(pl.multiple_of(ROWS + row, ROWS), ROWS)
            part = pl.ds(b * ROWS, ROWS)
            for t in range(2):
                total = terms[0, t, inner, :]
                for c in range(2):
                    value = datas[k][2 + c, t, part, :] * (datas[k][c, t, part, :] - surf[c, t, rows, :])
                    force[c, t, rows, :] = value
                    total = total + terms[1 + c, t, inner, :] * value
                grads[k][t, part, :] = total


def after_forcing(coef, s1, s2, s3, bottom, reach, force, out, n1, n2, n3, n4, work, sems):
    lane = lane_index()
    copies = []

    def send(l):
        for c in range(2):
            for t in range(2):
                source = n4.at[c * LAYERS + l, t, pl.ds(ROWS, TILE), :]
                target = out.at[c * LAYERS + l, :, pl.ds(t * LANES, LANES)]
                copy = pltpu.make_async_copy(source, target, sems.at[len(copies)])
                copy.start()
                copies.append(copy)

    for i in range(BLOCKS):
        rows, inner = pl.ds(ROWS + i * ROWS, ROWS), pl.ds(i * ROWS, ROWS)
        for t in range(2):
            for c in range(2):
                n4[c * LAYERS, t, rows, :] = bottom[c, t, rows, :] + reach[c, t, inner, :] * force[c, t, rows, :]
    send(0)

    def add_forcing(i, carry):
        rows = pl.ds(FIRST + i * ROWS, ROWS)
        for t in range(3):
            for c in range(2):
                value = coef[3, I0_ + c, t, rows, :] * force[c, t, rows, :]
                n1[c, t, rows, :] = s1[c * LAYERS + 3, t, rows, :] + value
                value = coef[2, I0_ + c, t, rows, :] * (coef[2, U_, t, rows, :] * value)
                n2[2 * c, t, rows, :] = s2[c * LAYERS + 2, t, rows, :] + value
                value = coef[1, I0_ + c, t, rows, :] * (coef[1, U_, t, rows, :] * value)
                n3[3 * c, t, rows, :] = s3[c * LAYERS + 1, t, rows, :] + value
        return carry

    lax.fori_loop(0, STEPS, add_forcing, 0, unroll=STEPS)

    def first(c, l):
        return n1.at[c] if l == 3 else s1.at[c * LAYERS + l]

    def second(c, l):
        return n2.at[2 * c + l - 2] if l >= 2 else s2.at[c * LAYERS + l]

    def third(c, l):
        return n3.at[3 * c + l - 1] if l >= 1 else s3.at[c * LAYERS + l]

    sweep_reached(coef, work, first, second, 3, lane, force)
    sweep_reached(coef, work, second, third, 2, lane)
    sweep_reached(coef, work, second, third, 3, lane, force)
    for l in (1, 2, 3):
        sweep_reached(coef, work, third, layers_of(n4), l, lane, force if l == 3 else None, last=True)
        send(l)
    for copy in copies:
        copy.wait()


def unpack_gradient(n, *refs):
    parts, out = refs[:n], refs[n]
    me = lax.axis_index("gy")
    for k in range(n):
        source = lax.rem(me + k, n)
        for t in range(2):
            out[:, pl.ds(pl.multiple_of(source * TILE + t * LANES, LANES), LANES)] = parts[k][t]


def f32(*shape):
    return jax.ShapeDtypeStruct(shape, jnp.float32)


def vmem_f32(*shape):
    return pltpu.VMEM(shape, jnp.float32)


def frames(*leading):
    return vmem_f32(*leading, 3, FRAME + ROWS, LANES)


def in_vmem(x):
    return pltpu.with_memory_space_constraint(x, pltpu.VMEM)


def in_hbm(x):
    return pltpu.with_memory_space_constraint(x, pltpu.HBM)


def per_device(
    adjoint_start,
    viscosity,
    base_velocity,
    surface_velocity,
    ice_mask,
    log_friction,
    observed_velocity,
    obs_weight,
):
    n = lax.axis_size("gy")
    size_x = lax.axis_size("gx")
    strip_rows = log_friction.shape[0]
    width = n * TILE
    vmem = pl.BlockSpec(memory_space=pltpu.VMEM)
    smem = pl.BlockSpec(memory_space=pltpu.SMEM)
    anywhere = pl.BlockSpec(memory_space=pl.ANY)
    ice_mask = in_hbm(ice_mask)
    adjoint = adjoint_start.reshape((2 * LAYERS, TILE, TILE))

    def params(mib):
        return pltpu.CompilerParams(vmem_limit_bytes=mib * MIB)

    def ring(k):
        return [(i, (i + k) % n) for i in range(n)]

    def line(size, k):
        return [(i, i + k) for i in range(size) if 0 <= i + k < size]

    def control_shape(k):
        return f32(control_rows(strip_rows) + (HALF if k in (1, n - 1) else 0), LANES)

    *controls, state, visc, surf = pl.pallas_call(
        functools.partial(pack_kernel, n, strip_rows),
        out_shape=[control_shape(k) for k in range(n)] + [frames(2 * LAYERS), frames(LAYERS), frames(2)],
        in_specs=[smem] + [anywhere] * 6,
        out_specs=[vmem] * (n + 3),
        scratch_shapes=[
            vmem_f32(strip_rows, width),
            vmem_f32(2, strip_rows, width),
            vmem_f32(2, strip_rows, width),
            pltpu.SemaphoreType.DMA((3 + 12 * CHUNKS,)),
        ],
        compiler_params=params(6),
    )(
        ice_mask,
        in_hbm(log_friction),
        in_hbm(observed_velocity),
        in_hbm(obs_weight),
        in_hbm(adjoint),
        in_hbm(viscosity),
        in_hbm(surface_velocity),
    )
    state, visc, surf = in_vmem(state), in_vmem(visc), in_vmem(surf)
    controls, observed_velocity, obs_weight = lax.optimization_barrier((controls, observed_velocity, obs_weight))
    datas = pl.pallas_call(
        functools.partial(pack_observations, n, strip_rows),
        out_shape=[f32(4, 2, strip_rows, LANES)] * n,
        in_specs=[anywhere] * 2,
        out_specs=[anywhere] * n,
        scratch_shapes=[vmem_f32(2, strip_rows, width)] * 2 + [pltpu.SemaphoreType.DMA((4 * n,))],
        compiler_params=params(8),
    )(in_hbm(observed_velocity), in_hbm(obs_weight))
    datas = list(datas)
    controls = [controls[0]] + [lax.ppermute(controls[k], "gy", ring(k)) for k in range(1, n)]
    controls, sent = lax.optimization_barrier((controls, datas[1:]))
    datas = [datas[0]] + [lax.ppermute(sent[k - 1], "gy", ring(k)) for k in range(1, n)]

    rows_up, rows_down = pl.pallas_call(
        functools.partial(pack_rows, n, strip_rows),
        out_shape=[f32(PAIRS, 3, ROWS, LANES)] * 2,
        in_specs=[smem] + [vmem] * (3 + n),
        out_specs=[vmem] * 2,
        scratch_shapes=[vmem_f32(2, 5, 3, ROWS, LANES)],
        compiler_params=params(4),
    )(ice_mask, state, visc, surf, *controls)
    above = lax.ppermute(rows_up, "gx", line(size_x, 1))
    below = lax.ppermute(rows_down, "gx", line(size_x, -1))

    held_shapes = [
        frames(LAYERS, 9),
        frames(2 * LAYERS),
        frames(2 * LAYERS),
        frames(2 * LAYERS),
        vmem_f32(2, 2, FRAME, LANES),
        vmem_f32(3, 2, TILE, LANES),
        vmem_f32(2, 2, TILE, LANES),
        frames(2),
        frames(),
        frames(),
        frames(),
    ]
    state, visc, surf, *held, bed = pl.pallas_call(
        functools.partial(before_forcing, n, strip_rows),
        out_shape=[frames(2 * LAYERS), frames(LAYERS), frames(2)] + held_shapes + [vmem_f32(2, 2, TILE, LANES)],
        in_specs=[smem] + [vmem] * 3 + [anywhere] + [vmem] * n,
        out_specs=[vmem] * 15,
        scratch_shapes=[pltpu.SemaphoreType.DMA((2,))],
        input_output_aliases={1: 0, 2: 1, 3: 2},
        compiler_params=params(6),
    )(ice_mask, state, visc, surf, in_hbm(base_velocity), *controls)
    edge_shapes = [frames(2 * LAYERS), frames(LAYERS)] + held_shapes
    _, _, *held = pl.pallas_call(
        functools.partial(at_edges, n),
        out_shape=edge_shapes,
        in_specs=[vmem] * (3 + len(edge_shapes)),
        out_specs=[vmem] * len(edge_shapes),
        input_output_aliases={3 + i: i for i in range(len(edge_shapes))},
        compiler_params=params(4),
    )(in_vmem(bed), above, below, *[in_vmem(x) for x in [state, visc] + held])
    coef, s1, s2, s3, bottom, terms, reach, force = [in_vmem(x) for x in held[:8]]

    force, *grads = pl.pallas_call(
        functools.partial(gradient_kernel, n, strip_rows),
        out_shape=[frames(2)] + [f32(2, strip_rows, LANES)] * n,
        in_specs=[vmem] * (3 + n),
        out_specs=[vmem] * (1 + n),
        input_output_aliases={2: 0},
        compiler_params=params(6),
    )(terms, in_vmem(surf), in_vmem(force), *datas)
    parts = [grads[0]] + [lax.ppermute(grads[k], "gy", ring(n - k)) for k in range(1, n)]

    out = pl.pallas_call(
        after_forcing,
        out_shape=f32(2 * LAYERS, TILE, TILE),
        in_specs=[vmem] * 7,
        out_specs=anywhere,
        scratch_shapes=[
            frames(2),
            frames(4),
            frames(6),
            vmem_f32(2 * LAYERS, 2, FRAME, LANES),
            frames(2, 2),
            pltpu.SemaphoreType.DMA((16,)),
        ],
        compiler_params=params(18),
    )(coef, s1, s2, s3, bottom, reach, in_vmem(force))

    gradient = pl.pallas_call(
        functools.partial(unpack_gradient, n),
        out_shape=f32(strip_rows, width),
        in_specs=[vmem] * n,
        out_specs=vmem,
        compiler_params=params(4),
    )(*parts)
    return gradient, out.reshape(adjoint_start.shape)


def solution(mesh):
    placed = (
        P(None, None, "gx", "gy"),
        P(None, "gx", "gy"),
        P(None, "gx", "gy"),
        P(None, "gx", "gy"),
        P("gx", "gy"),
        P(("gx", "gy"), None),
        P(None, ("gx", "gy"), None),
        P(None, ("gx", "gy"), None),
    )
    return jax.shard_map(
        per_device,
        mesh=mesh,
        in_specs=placed,
        out_specs=(P(("gx", "gy"), None), P(None, None, "gx", "gy")),
        check_vma=False,
    )
```
